256 devices in a mesh: row: 16 (over x, z_lo, core), col: 16 (over y, z_hi).
Axes of the slice: x: 4, y: 4, z: 8 (z_hi: 4, z_lo: 2; z = z_hi * 2 + z_lo), core: 2. Of those that a mesh axis runs over, the one named last changes fastest.
Arguments:
- obj: float32 [2, 2, 4096, 4096], P(None, None, 'row', 'col'), may hold values from -1.5 to 1.5
- probe: float32 [2, 256, 256], replicated, may hold values from -5 to 5
- amplitude: float32 [16, 16, 2, 1, 256, 256], P('row', 'col'), may hold values from 0 to 2
- positions: int32 [16, 16, 2, 1, 2], P('row', 'col'), may hold values from 0 to 256
Outputs:
- updated: float32 [2, 2, 4096, 4096], P(None, None, 'row', 'col')
The draws below stay inside these ranges and needn't reach their ends.
Inputs may be any that keep to these rules, and one draw needn't show every extreme that they name: `positions`: every probe window lies inside its tile's region widened by 128 pixels on each side.
All inputs are finite; a program needn't handle non-finite values.
Results may differ from the reference program's by a relative error of at most 0.0003.
Values sent between devices are 32-bit elements; how exact they have to be, the bound alone decides.
A program may use at most 64 MiB of HBM per device.

```python
import math
import jax
import jax.numpy as jnp
from jax import lax

TILE = 256
MARGIN = 128
PROBES = 1
HEIGHT = 4096
WIDTH = 4096
N_ROW = 16
N_COL = 16


def plant(values, own_key, least, high):
    place = [jax.random.randint(jax.random.fold_in(own_key, axis), (), 0, length) for axis, length in enumerate(values.shape)]
    longest = values.shape.index(max(values.shape))
    next_to = place[:longest] + [(place[longest] + 1) % values.shape[longest]] + place[longest + 1:]
    return values.at[tuple(place)].set(least).at[tuple(next_to)].set(high)


def level_of(key, extent, cuts, low, high):
    gain = 1.0
    for dim, shards_of in cuts:
        heights = jax.random.uniform(jax.random.fold_in(jax.random.fold_in(key, 6), dim), (shards_of,), jnp.float32, low / len(cuts), high / len(cuts))
        gain = gain * jnp.repeat(jnp.exp(heights), extent[dim] // shards_of).reshape((-1,) + (1,) * (len(extent) - 1 - dim))
    return gain


def bell_draw(rng, dims, scale, reach, pieces=(), kind=jnp.bfloat16):
    values = jax.random.normal(rng, dims, jnp.float32) * scale
    if len(pieces) > 0:
        values = level_of(rng, dims, pieces, -0.22, 0.18) * values
    return jnp.clip(values, min=-reach, max=reach).astype(kind)


def setup_inputs(seed: int = 0) -> dict:
    arg_keys = jax.random.split(jax.random.key(seed), 5)
    return {
        "obj": bell_draw(arg_keys[0], (2, 2, HEIGHT, WIDTH), 0.3, 1.5, ((2, 16), (3, 16)), jnp.float32),
        "probe": bell_draw(arg_keys[1], (2, TILE, TILE), 1.0, 5.0, (), jnp.float32),
        "amplitude": jnp.clip(2.0 * jax.random.uniform(arg_keys[2], (N_ROW, N_COL, 2, PROBES, TILE, TILE), jnp.float32) ** level_of(arg_keys[2], (N_ROW, N_COL, 2, PROBES, TILE, TILE), ((0, 16), (1, 16)), -0.2, 0.2), 0.0, 2.0),
        "positions": plant(jax.random.randint(arg_keys[3], (N_ROW, N_COL, 2, PROBES, 2), 0, 2 * MARGIN + 1), jax.random.fold_in(arg_keys[3], 1), 0, 2 * MARGIN).astype(jnp.int32),
    }


step_size = 0.5

def fresnel(size):
    index = jnp.arange(size, dtype=jnp.int32)
    freq = jnp.where(index < size // 2, index, index - size)
    square = (freq[:, None] * freq[:, None] + freq[None, :] * freq[None, :]) % (4 * size)
    phase = math.pi / (2 * size) * square.astype(jnp.float32)
    return jnp.cos(phase) - 1j * jnp.sin(phase)

def probe_gradient(padded_object, exit_wave, propagation_kernel, top_row, left_column, measured):
    zero = jnp.zeros((), jnp.int32)
    patch = lax.dynamic_slice(padded_object, (zero, zero, top_row.astype(jnp.int32), left_column.astype(jnp.int32)), (2, 2, TILE, TILE))
    first = 1.0 + patch[0, 0] + 1j * patch[0, 1]
    second = 1.0 + patch[1, 0] + 1j * patch[1, 1]
    entry = exit_wave * first
    inner = jnp.fft.ifft2(propagation_kernel * jnp.fft.fft2(entry, norm='ortho'), norm='ortho')
    leaving = inner * second
    far = jnp.fft.fft2(leaving, norm='ortho')
    power = far.real * far.real + far.imag * far.imag
    resid = far - measured * far / jnp.sqrt(power + 1.0)
    chi = jnp.fft.ifft2(resid, norm='ortho')
    grad_two = jnp.conj(inner) * chi
    back = jnp.conj(second) * chi
    back = jnp.fft.ifft2(jnp.conj(propagation_kernel) * jnp.fft.fft2(back, norm='ortho'), norm='ortho')
    grad_one = jnp.conj(exit_wave) * back
    return jnp.stack([jnp.stack([grad_one.real, grad_one.imag]), jnp.stack([grad_two.real, grad_two.imag])])

def reference(obj, probe, amplitude, positions):
    padded_object = jnp.pad(obj, ((0, 0), (0, 0), (MARGIN, MARGIN), (MARGIN, MARGIN)))
    propagation_kernel = fresnel(TILE)
    exit_wave = probe[0] + 1j * probe[1]
    result = obj
    for batch in range(2):
        tops = (jnp.arange(N_ROW, dtype=jnp.int32) * TILE)[:, None, None] + positions[:, :, batch, :, 0]
        lefts = (jnp.arange(N_COL, dtype=jnp.int32) * TILE)[None, :, None] + positions[:, :, batch, :, 1]
        tops = tops.reshape(-1).astype(jnp.int32)
        lefts = lefts.reshape(-1).astype(jnp.int32)
        measured = amplitude[:, :, batch].reshape(-1, TILE, TILE)

        def add_one(total, scan_entry):
            top_row, left_column, measured_intensity = scan_entry
            object_gradient = probe_gradient(padded_object, exit_wave, propagation_kernel, top_row, left_column, measured_intensity)
            zero = jnp.zeros((), jnp.int32)
            start = (zero, zero, top_row, left_column)
            current = lax.dynamic_slice(total, start, (2, 2, TILE, TILE))
            return (lax.dynamic_update_slice(total, current + object_gradient.astype(total.dtype), start), None)
        total, unused = lax.scan(add_one, jnp.zeros_like(padded_object), (tops, lefts, measured))
        result = result - step_size * total[:, :, MARGIN:MARGIN + HEIGHT, MARGIN:MARGIN + WIDTH]
    return result
```

```python
import functools
import math

import jax
import jax.numpy as jnp
import numpy as np
from jax import lax
from jax.experimental import pallas as pl
from jax.experimental.pallas import tpu as pltpu
from jax.sharding import PartitionSpec as P

TILE = 256
MARGIN = 128
HALF = 128
WIDE = 512
STEP = 0.5
MESH = pl.DeviceIdType.MESH

G_FX, G_FI, G_VX, G_VI, G_CROSS, G_CROSS2, G_DIRECT, G_FWD, G_IN, G_IN2, G_INF, G_INV = range(12)
S_CROSS, S_DIRECT, S_IN, S_FX, S_FI, S_VX, S_VI = range(7)

T_A, T_F, T_FI, T_AC = range(4)


def real_form(m):
    return np.block([[m.real, m.imag], [-m.imag, m.real]])


def matrices():
    n = np.arange(TILE)
    f = np.where(n < TILE // 2, n, n - TILE)
    h = np.exp(-1j * math.pi * ((f * f) % (4 * TILE)) / (2 * TILE))
    dft = np.exp(-2j * math.pi * ((n[:, None] * n[None, :]) % TILE) / TILE) / math.sqrt(TILE)
    spread = np.conj(dft) @ (h[:, None] * dft)
    c0, c1 = spread[:HALF, :HALF], spread[:HALF, HALF:]
    a = [(c0 + c1) / 2, (c0 - c1) / 2]
    fwd = [dft[:HALF, 0::2], dft[:HALF, 1::2]]
    inv = [np.conj(m.T) for m in fwd]
    ac = [np.conj(m) for m in a]
    return np.stack([np.stack([real_form(m) for m in pair]) for pair in (a, fwd, inv, ac)])


def constants():
    right = matrices()
    both = np.stack([right, np.swapaxes(right, -1, -2)], 2)
    both = both.astype(np.float32)
    high = both.astype(jnp.bfloat16)
    low = (both - high.astype(np.float32)).astype(jnp.bfloat16)
    mats = np.stack([high, low], 3)
    order = np.concatenate([np.arange(0, TILE, 2), np.arange(1, TILE, 2)])
    perm = np.zeros((TILE, TILE), np.float32)
    perm[order, np.arange(TILE)] = 1.0
    perms = np.stack([perm, perm.T]).astype(jnp.bfloat16)
    return mats, perms


def split(x):
    high = x.astype(jnp.bfloat16)
    low = (x - high.astype(jnp.float32)).astype(jnp.bfloat16)
    return high, low


def dot(a, b):
    return jnp.dot(a, b, preferred_element_type=jnp.float32)


def mm_right(x, high, low):
    xh, xl = split(x)
    return dot(xh, high) + (dot(xl, high) + dot(xh, low))


def mm_left(high, low, x):
    xh, xl = split(x)
    return dot(high, xh) + (dot(high, xl) + dot(low, xh))


def transform(src, mid, dst, mats, which, pre, post):
    def one(w, carry):
        xr, xi = src[w, 0], src[w, 1]
        r0, r1, i0, i1 = xr[:, :HALF], xr[:, HALF:], xi[:, :HALF], xi[:, HALF:]
        if pre:
            r0, r1, i0, i1 = r0 + r1, r0 - r1, i0 + i1, i0 - i1
        ys = mm_right(jnp.concatenate([r0, i0], 1), mats[which, 0, 0, 0], mats[which, 0, 0, 1])
        yd = mm_right(jnp.concatenate([r1, i1], 1), mats[which, 1, 0, 0], mats[which, 1, 0, 1])
        if post:
            ys, yd = ys + yd, ys - yd
        yr = jnp.concatenate([ys[:, :HALF], yd[:, :HALF]], 1)
        yi = jnp.concatenate([ys[:, HALF:], yd[:, HALF:]], 1)
        r0, r1, i0, i1 = yr[:HALF], yr[HALF:], yi[:HALF], yi[HALF:]
        if pre:
            r0, r1, i0, i1 = r0 + r1, r0 - r1, i0 + i1, i0 - i1
        zs = mm_left(mats[which, 0, 1, 0], mats[which, 0, 1, 1], jnp.concatenate([r0, i0], 0))
        zd = mm_left(mats[which, 1, 1, 0], mats[which, 1, 1, 1], jnp.concatenate([r1, i1], 0))
        if post:
            zs, zd = zs + zd, zs - zd
        dst[w, 0, :HALF, :] = zs[:HALF]
        dst[w, 0, HALF:, :] = zd[:HALF]
        dst[w, 1, :HALF, :] = zs[HALF:]
        dst[w, 1, HALF:, :] = zd[HALF:]
        return carry

    lax.fori_loop(0, 2, one, 0)


ROWS = 32


def rows_loop(count, fn):
    def step(k, carry):
        fn(pl.multiple_of(k * ROWS, ROWS))
        return carry

    lax.fori_loop(0, count // ROWS, step, 0)


def kernel(
    n_row, n_col,
    pos_ref, obj_ref, probe_ref, amp_ref, mats_ref, perms_ref,
    out_ref,
    pad0, pad1, tot0, tot1, gbuf, probe, amp, mats, perms, amp_p, x_ref, b_ref, t_ref, mid,
    r_in, r_x, r_d, r_f, r_v,
    local_sem, g_send, g_recv, s_send, s_recv,
):
    i, j = lax.axis_index("row"), lax.axis_index("col")
    core = lax.rem(i, 2)
    c = lax.rem(lax.div(i, 2), 2)
    i_in = i + 1 - 2 * core
    i_x = i - 1 + 2 * core
    j_v = j - 1 + 2 * c
    j_f = j + 1 - 2 * c
    has_x = jnp.logical_and(i_x >= 0, i_x < n_row)
    has_v = jnp.logical_and(j_v >= 0, j_v < n_col)
    has_f = jnp.logical_and(j_f >= 0, j_f < n_col)
    has_d = jnp.logical_and(has_x, has_v)
    ix = jnp.clip(i_x, 0, n_row - 1)
    jv = jnp.clip(j_v, 0, n_col - 1)
    jf = jnp.clip(j_f, 0, n_col - 1)
    always = None
    pads, tots = (pad0, pad1), (tot0, tot1)

    def at(start):
        return pl.ds(pl.multiple_of(start, HALF), HALF)

    x_rows, in_rows = at(HALF * core), at(HALF * (1 - core))
    x_rows_p, in_rows_p = at(MARGIN + HALF * core), at(MARGIN + HALF * (1 - core))

    border = jnp.logical_not(jnp.logical_and(has_x, jnp.logical_and(has_v, has_f)))

    @pl.when(border)
    def _():
        def zero(r):
            for pad in pads:
                pad[:, :, pl.ds(r, ROWS), :] = jnp.zeros((2, 4, ROWS, HALF), jnp.float32)

        rows_loop(WIDE, zero)

    barrier = pltpu.get_barrier_semaphore()

    def when(cond, fn):
        if cond is None:
            fn()
        else:
            pl.when(cond)(fn)

    partners = ((None, (i_in, j)), (has_x, (ix, j)), (has_d, (ix, jv)), (has_v, (i, jv)), (has_f, (i, jf)))
    for cond, dev in partners:
        when(cond, lambda dev=dev: pl.semaphore_signal(barrier, inc=1, device_id=dev, device_id_type=MESH))
    one = lambda cond: cond.astype(jnp.int32)
    pl.semaphore_wait(barrier, 1 + one(has_x) + one(has_d) + one(has_v) + one(has_f))

    def gather(s):
        pad = pads[s]
        dst_x, dst_in = at(3 * HALF * (1 - core)), at(3 * HALF * core)
        f_src, f_dst = at(HALF * (1 - c)), 3 * c
        v_src, v_dst = at(HALF * c), 3 * (1 - c)
        west, east = pl.ds(0, HALF), pl.ds(HALF, HALF)
        obj = obj_ref.at[s]
        table = {
            G_FX: (has_f, has_v, obj.at[:, x_rows, f_src], pad.at[:, f_dst, x_rows_p, :], (i, jf)),
            G_FI: (has_f, has_v, obj.at[:, in_rows, f_src], pad.at[:, f_dst, in_rows_p, :], (i, jf)),
            G_VX: (has_v, has_f, obj.at[:, x_rows, v_src], pad.at[:, v_dst, x_rows_p, :], (i, jv)),
            G_VI: (has_v, has_f, obj.at[:, in_rows, v_src], pad.at[:, v_dst, in_rows_p, :], (i, jv)),
            G_CROSS: (has_x, has_x, obj.at[:, x_rows, west], pad.at[:, 1, dst_x, :], (ix, j)),
            G_CROSS2: (has_x, has_x, obj.at[:, x_rows, east], pad.at[:, 2, dst_x, :], (ix, j)),
            G_DIRECT: (has_d, has_d, obj.at[:, x_rows, v_src], pad.at[:, v_dst, dst_x, :], (ix, jv)),
            G_FWD: (has_x, has_x, pad.at[:, f_dst, x_rows_p, :], pad.at[:, f_dst, dst_x, :], (ix, j)),
            G_IN: (always, always, obj.at[:, in_rows, west], pad.at[:, 1, dst_in, :], (i_in, j)),
            G_IN2: (always, always, obj.at[:, in_rows, east], pad.at[:, 2, dst_in, :], (i_in, j)),
            G_INF: (always, always, pad.at[:, f_dst, in_rows_p, :], pad.at[:, f_dst, dst_in, :], (i_in, j)),
            G_INV: (always, always, pad.at[:, v_dst, in_rows_p, :], pad.at[:, v_dst, dst_in, :], (i_in, j)),
        }
        return {
            k: (sent, comes, pltpu.make_async_remote_copy(
                src_ref=src, dst_ref=dst, send_sem=g_send.at[s, k], recv_sem=g_recv.at[s, k],
                device_id=dev, device_id_type=MESH))
            for k, (sent, comes, src, dst, dev) in table.items()
        }

    def start(copies, *keys):
        for k in keys:
            sent, _, copy = copies[k]
            when(sent, copy.start)

    def arrived(copies, *keys):
        for k in keys:
            _, comes, copy = copies[k]
            when(comes, copy.wait_recv)

    def left(copies, *keys):
        for k in keys:
            sent, _, copy = copies[k]
            when(sent, copy.wait_send)

    g0, g1 = gather(0), gather(1)
    first = (G_FX, G_CROSS, G_CROSS2, G_FI, G_VI, G_VX, G_DIRECT, G_IN, G_IN2)
    start(g0, *first)

    inner = pl.ds(MARGIN, TILE)
    locals_ = [
        pltpu.make_async_copy(obj_ref.at[s, :, :, pl.ds(HALF * k, HALF)], pad.at[:, 1 + k, inner, :], local_sem.at[4 + 2 * s + k])
        for s, pad in enumerate(pads)
        for k in range(2)
    ] + [
        pltpu.make_async_copy(probe_ref, probe, local_sem.at[0]),
        pltpu.make_async_copy(amp_ref, amp, local_sem.at[1]),
        pltpu.make_async_copy(mats_ref, mats, local_sem.at[2]),
        pltpu.make_async_copy(perms_ref, perms, local_sem.at[3]),
    ]
    for copy in locals_:
        copy.start()

    start(g1, *first)

    def clear(r):
        for w in range(2):
            gbuf[w, :, :, pl.ds(r, ROWS), :] = jnp.zeros((2, 5, ROWS, HALF), jnp.float32)

    rows_loop(3 * TILE, clear)
    for copy in locals_[5:]:
        copy.wait()

    def order(w, carry):
        rest = amp[w]
        total = None
        for _ in range(3):
            piece = rest.astype(jnp.bfloat16)
            rest = rest - piece.astype(jnp.float32)
            part = dot(perms[1], dot(piece, perms[0]).astype(jnp.bfloat16))
            total = part if total is None else total + part
        amp_p[w] = total
        return carry

    lax.fori_loop(0, 2, order, 0)
    for copy in locals_[:5]:
        copy.wait()

    lane = lax.broadcasted_iota(jnp.int32, (ROWS, HALF), 1)

    def place(w):
        y, x = pos_ref[2 * w], pos_ref[2 * w + 1]
        q = jnp.minimum(lax.div(x, HALF), 1)
        return y, q, x - q * HALF

    def window(pad, w, part, r):
        y, block, s = place(w)
        turn = lax.rem(HALF - s, HALF)
        v = [pltpu.roll(pad[part, block + k, pl.ds(y + r, ROWS), :], turn, 1) for k in range(3)]
        own = lane < HALF - s
        return jnp.concatenate([jnp.where(own, v[0], v[1]), jnp.where(own, v[1], v[2])], 1)

    def finish_gather(copies):
        arrived(copies, G_FX)
        start(copies, G_FWD)
        arrived(copies, G_FI)
        start(copies, G_INF)
        arrived(copies, G_VI)
        start(copies, G_INV)
        arrived(copies, G_VX, G_CROSS, G_CROSS2, G_DIRECT, G_IN, G_IN2, G_FWD, G_INF, G_INV)

    finish_gather(g0)

    for w in range(2):
        def enter(r, w=w):
            rows = pl.ds(r, ROWS)
            tr, ti = 1.0 + window(pad0, w, 0, r), window(pad0, w, 1, r)
            pr, pi = probe[0, rows, :], probe[1, rows, :]
            x_ref[w, 0, rows, :] = pr * tr - pi * ti
            x_ref[w, 1, rows, :] = pr * ti + pi * tr

        rows_loop(TILE, enter)
    transform(x_ref, mid, b_ref, mats, T_A, True, True)

    finish_gather(g1)

    for w in range(2):
        def leave(r, w=w):
            rows = pl.ds(r, ROWS)
            tr, ti = 1.0 + window(pad1, w, 0, r), window(pad1, w, 1, r)
            t_ref[w, 0, rows, :] = tr
            t_ref[w, 1, rows, :] = ti
            br, bi = b_ref[w, 0, rows, :], b_ref[w, 1, rows, :]
            x_ref[w, 0, rows, :] = br * tr - bi * ti
            x_ref[w, 1, rows, :] = br * ti + bi * tr

        rows_loop(TILE, leave)
    transform(x_ref, mid, x_ref, mats, T_F, True, False)

    for w in range(2):
        def residual(r, w=w):
            rows = pl.ds(r, ROWS)
            fr, fi = x_ref[w, 0, rows, :], x_ref[w, 1, rows, :]
            keep = 1.0 - amp_p[w, rows, :] * lax.rsqrt(fr * fr + fi * fi + 1.0)
            x_ref[w, 0, rows, :] = fr * keep
            x_ref[w, 1, rows, :] = fi * keep

        rows_loop(TILE, residual)
    transform(x_ref, mid, x_ref, mats, T_FI, False, True)

    def turned(w, part, r, v):
        _, _, s = place(w)
        turn = lax.rem(s, HALF)
        a, b = (pltpu.roll(v[:, HALF * k : HALF * (k + 1)], turn, 1) for k in range(2))
        own = lane >= s
        rows = pl.ds(TILE + r, ROWS)
        gbuf[w, part, 1, rows, :] = jnp.where(own, a, 0.0)
        gbuf[w, part, 2, rows, :] = jnp.where(own, b, a)
        gbuf[w, part, 3, rows, :] = jnp.where(own, 0.0, b)

    def add_up(tot):
        def chunk(r):
            for part in range(2):
                for k in range(4):
                    total = None
                    for w in range(2):
                        y, block, _ = place(w)
                        v = gbuf[w, part, 1 - block + k, pl.ds(TILE - y + r, ROWS), :]
                        total = v if total is None else total + v
                    tot[part, k, pl.ds(r, ROWS), :] = total

        rows_loop(WIDE, chunk)

    def scatter(s):
        tot = tots[s]
        cross_rows, inner_rows = at(3 * HALF * core), at(3 * HALF * (1 - core))
        f_blk, v_blk = 3 * (1 - c), 3 * c
        table = {
            S_CROSS: (has_x, has_x, tot.at[:, pl.ds(1 - c, 3), cross_rows, :], r_x.at[s], (ix, j)),
            S_DIRECT: (has_d, has_d, tot.at[:, v_blk, cross_rows, :], r_d.at[s], (ix, jv)),
            S_IN: (always, always, tot.at[:, :, inner_rows, :], r_in.at[s], (i_in, j)),
            S_FX: (has_f, has_v, tot.at[:, f_blk, x_rows_p, :], r_f.at[s, :, x_rows, :], (i, jf)),
            S_FI: (has_f, has_v, tot.at[:, f_blk, in_rows_p, :], r_f.at[s, :, in_rows, :], (i, jf)),
            S_VX: (has_v, has_f, tot.at[:, v_blk, x_rows_p, :], r_v.at[s, :, x_rows, :], (i, jv)),
            S_VI: (has_v, has_f, tot.at[:, v_blk, in_rows_p, :], r_v.at[s, :, in_rows, :], (i, jv)),
        }
        return {
            k: (sent, comes, pltpu.make_async_remote_copy(
                src_ref=src, dst_ref=dst, send_sem=s_send.at[s, k], recv_sem=s_recv.at[s, k],
                device_id=dev, device_id_type=MESH))
            for k, (sent, comes, src, dst, dev) in table.items()
        }

    def add_in(s):
        tot = tots[s]

        def chunk(r):
            rows = pl.ds(pl.multiple_of(MARGIN + HALF * (1 - core) + r, ROWS), ROWS)
            tot[:, :, rows, :] = tot[:, :, rows, :] + r_in[s, :, :, pl.ds(r, ROWS), :]

        rows_loop(HALF, chunk)

    def add_cross(s):
        tot = tots[s]
        blks = pl.ds(c, 3)

        def chunk(r):
            rows = pl.ds(pl.multiple_of(MARGIN + HALF * core + r, ROWS), ROWS)
            tot[:, blks, rows, :] = tot[:, blks, rows, :] + r_x[s, :, :, pl.ds(r, ROWS), :]

        @pl.when(has_x)
        def _():
            rows_loop(HALF, chunk)

    def send_early(s, copies):
        start(copies, S_CROSS, S_IN, S_FX, S_DIRECT)

    def send_inner(s, copies):
        arrived(copies, S_IN)
        add_in(s)
        start(copies, S_FI, S_VI)

    def send_late(s, copies):
        arrived(copies, S_CROSS)
        add_cross(s)
        start(copies, S_VX)

    def finish(s, copies):
        tot = tots[s]
        arrived(copies, S_DIRECT, S_FX, S_FI, S_VX, S_VI)

        def add(cond, count, first_row, blk, buf):
            def chunk(r):
                rows = pl.ds(pl.multiple_of(first_row + r, ROWS), ROWS)
                tot[:, blk, rows, :] = tot[:, blk, rows, :] + buf[s, :, pl.ds(r, ROWS), :]

            @pl.when(cond)
            def _():
                rows_loop(count, chunk)

        add(has_d, HALF, MARGIN + HALF * core, 1 + c, r_d)
        add(has_v, TILE, MARGIN, 1 + c, r_f)
        add(has_f, TILE, MARGIN, 2 - c, r_v)

        def chunk(r):
            for k in range(2):
                out_ref[s, :, pl.ds(r, ROWS), HALF * k : HALF * (k + 1)] = tot[:, 1 + k, pl.ds(MARGIN + r, ROWS), :]

        rows_loop(TILE, chunk)

    for w in range(2):
        def second(r, w=w):
            rows = pl.ds(r, ROWS)
            br, bi = b_ref[w, 0, rows, :], b_ref[w, 1, rows, :]
            cr, ci = x_ref[w, 0, rows, :], x_ref[w, 1, rows, :]
            turned(w, 0, r, br * cr + bi * ci)
            turned(w, 1, r, br * ci - bi * cr)

        rows_loop(TILE, second)
    add_up(tot1)
    s1 = scatter(1)
    send_early(1, s1)

    for w in range(2):
        def back(r, w=w):
            rows = pl.ds(r, ROWS)
            tr, ti = t_ref[w, 0, rows, :], t_ref[w, 1, rows, :]
            cr, ci = x_ref[w, 0, rows, :], x_ref[w, 1, rows, :]
            x_ref[w, 0, rows, :] = tr * cr + ti * ci
            x_ref[w, 1, rows, :] = tr * ci - ti * cr

        rows_loop(TILE, back)
    send_inner(1, s1)
    transform(x_ref, mid, x_ref, mats, T_AC, True, True)
    for w in range(2):
        def first_slice(r, w=w):
            rows = pl.ds(r, ROWS)
            pr, pi = probe[0, rows, :], probe[1, rows, :]
            cr, ci = x_ref[w, 0, rows, :], x_ref[w, 1, rows, :]
            turned(w, 0, r, pr * cr + pi * ci)
            turned(w, 1, r, pr * ci - pi * cr)

        rows_loop(TILE, first_slice)
    add_up(tot0)
    s0 = scatter(0)
    send_early(0, s0)
    send_inner(0, s0)
    send_late(1, s1)
    send_late(0, s0)
    finish(1, s1)
    finish(0, s0)
    for copies in (g0, g1, s0, s1):
        left(copies, *copies)


def body(n_row, n_col, mats, perms, obj, probe, amplitude, positions):
    any_space = pl.BlockSpec(memory_space=pl.ANY)
    vmem = pl.BlockSpec(memory_space=pltpu.VMEM)
    smem = pl.BlockSpec(memory_space=pltpu.SMEM)
    f32 = jnp.float32
    wide = pltpu.VMEM((2, 4, WIDE, HALF), f32)
    field = pltpu.VMEM((2, 2, TILE, TILE), f32)
    gradient = pl.pallas_call(
        functools.partial(kernel, n_row, n_col),
        out_shape=jax.ShapeDtypeStruct((2, 2, TILE, TILE), f32),
        in_specs=[smem] + [any_space] * 5,
        out_specs=vmem,
        scratch_shapes=[
            wide, wide, wide, wide,
            pltpu.VMEM((2, 2, 5, 3 * TILE, HALF), f32),
            pltpu.VMEM((2, TILE, TILE), f32),
            pltpu.VMEM((2, TILE, TILE), f32),
            pltpu.VMEM(mats.shape, jnp.bfloat16),
            pltpu.VMEM(perms.shape, jnp.bfloat16),
            pltpu.VMEM((2, TILE, TILE), f32),
            field, field, field,
            pltpu.VMEM((2, TILE, TILE), f32),
            pltpu.VMEM((2, 2, 4, HALF, HALF), f32),
            pltpu.VMEM((2, 2, 3, HALF, HALF), f32),
            pltpu.VMEM((2, 2, HALF, HALF), f32),
            pltpu.VMEM((2, 2, TILE, HALF), f32),
            pltpu.VMEM((2, 2, TILE, HALF), f32),
            pltpu.SemaphoreType.DMA((8,)),
            pltpu.SemaphoreType.DMA((2, 12)),
            pltpu.SemaphoreType.DMA((2, 12)),
            pltpu.SemaphoreType.DMA((2, 7)),
            pltpu.SemaphoreType.DMA((2, 7)),
        ],
        compiler_params=pltpu.CompilerParams(
            collective_id=0, has_side_effects=True, vmem_limit_bytes=56 * 1024 * 1024
        ),
        cost_estimate=pl.CostEstimate(flops=3 * 10**9, bytes_accessed=8 * 10**6, transcendentals=131072),
    )(positions.reshape(4), obj, probe, amplitude.reshape(2, TILE, TILE), mats, perms)
    return obj - STEP * gradient


def solution(mesh):
    mats, perms = constants()
    mats, perms = jnp.asarray(mats), jnp.asarray(perms)
    placed = (
        P(None, None, "row", "col"),
        P(),
        P("row", "col", None, None, None, None),
        P("row", "col", None, None, None),
    )
    return jax.shard_map(
        functools.partial(body, mesh.shape["row"], mesh.shape["col"], mats, perms),
        mesh=mesh, in_specs=placed, out_specs=P(None, None, "row", "col"), check_vma=False,
    )
```

```python
import functools
import math

import jax
import jax.numpy as jnp
import numpy as np
from jax import lax
from jax.experimental import pallas as pl
from jax.experimental.pallas import tpu as pltpu
from jax.sharding import PartitionSpec as P

TILE = 256
MARGIN = 128
HALF = 128
WIDE = 512
STEP = 0.5
MESH = pl.DeviceIdType.MESH

G_FX, G_FI, G_VX, G_VI, G_CROSS, G_CROSS2, G_DIRECT, G_FWD, G_IN, G_IN2, G_INF, G_INV = range(12)
S_CORNER, S_CROSS, S_DIRECT, S_IN, S_FX, S_FI, S_VX, S_VI = range(8)

T_A, T_F, T_FI, T_AC = range(4)


def real_form(m):
    return np.block([[m.real, m.imag], [-m.imag, m.real]])


def matrices():
    n = np.arange(TILE)
    f = np.where(n < TILE // 2, n, n - TILE)
    h = np.exp(-1j * math.pi * ((f * f) % (4 * TILE)) / (2 * TILE))
    dft = np.exp(-2j * math.pi * ((n[:, None] * n[None, :]) % TILE) / TILE) / math.sqrt(TILE)
    spread = np.conj(dft) @ (h[:, None] * dft)
    c0, c1 = spread[:HALF, :HALF], spread[:HALF, HALF:]
    a = [(c0 + c1) / 2, (c0 - c1) / 2]
    fwd = [dft[:HALF, 0::2], dft[:HALF, 1::2]]
    inv = [np.conj(m.T) for m in fwd]
    ac = [np.conj(m) for m in a]
    return np.stack([np.stack([real_form(m) for m in pair]) for pair in (a, fwd, inv, ac)])


def constants():
    right = matrices()
    both = np.stack([right, np.swapaxes(right, -1, -2)], 2)
    both = both.astype(np.float32)
    high = both.astype(jnp.bfloat16)
    low = (both - high.astype(np.float32)).astype(jnp.bfloat16)
    mats = np.stack([high, low], 3)
    order = np.concatenate([np.arange(0, TILE, 2), np.arange(1, TILE, 2)])
    perm = np.zeros((TILE, TILE), np.float32)
    perm[order, np.arange(TILE)] = 1.0
    perms = np.stack([perm, perm.T]).astype(jnp.bfloat16)
    return mats, perms


def split(x):
    high = x.astype(jnp.bfloat16)
    low = (x - high.astype(jnp.float32)).astype(jnp.bfloat16)
    return high, low


def dot(a, b):
    return jnp.dot(a, b, preferred_element_type=jnp.float32)


def mm_right(x, high, low):
    xh, xl = split(x)
    return dot(xh, high) + (dot(xl, high) + dot(xh, low))


def mm_left(high, low, x):
    xh, xl = split(x)
    return dot(high, xh) + (dot(high, xl) + dot(low, xh))


def transform(src, dst, mats, which, pre, post):
    def one(w, carry):
        xr, xi = src[w, 0], src[w, 1]
        r0, r1, i0, i1 = xr[:, :HALF], xr[:, HALF:], xi[:, :HALF], xi[:, HALF:]
        if pre:
            r0, r1, i0, i1 = r0 + r1, r0 - r1, i0 + i1, i0 - i1
        ys = mm_right(jnp.concatenate([r0, i0], 1), mats[which, 0, 0, 0], mats[which, 0, 0, 1])
        yd = mm_right(jnp.concatenate([r1, i1], 1), mats[which, 1, 0, 0], mats[which, 1, 0, 1])
        if post:
            ys, yd = ys + yd, ys - yd
        yr = jnp.concatenate([ys[:, :HALF], yd[:, :HALF]], 1)
        yi = jnp.concatenate([ys[:, HALF:], yd[:, HALF:]], 1)
        r0, r1, i0, i1 = yr[:HALF], yr[HALF:], yi[:HALF], yi[HALF:]
        if pre:
            r0, r1, i0, i1 = r0 + r1, r0 - r1, i0 + i1, i0 - i1
        zs = mm_left(mats[which, 0, 1, 0], mats[which, 0, 1, 1], jnp.concatenate([r0, i0], 0))
        zd = mm_left(mats[which, 1, 1, 0], mats[which, 1, 1, 1], jnp.concatenate([r1, i1], 0))
        if post:
            zs, zd = zs + zd, zs - zd
        dst[w, 0, :HALF, :] = zs[:HALF]
        dst[w, 0, HALF:, :] = zd[:HALF]
        dst[w, 1, :HALF, :] = zs[HALF:]
        dst[w, 1, HALF:, :] = zd[HALF:]
        return carry

    lax.fori_loop(0, 2, one, 0)


ROWS = 32


def rows_loop(count, fn):
    def step(k, carry):
        fn(pl.multiple_of(k * ROWS, ROWS))
        return carry

    lax.fori_loop(0, count // ROWS, step, 0)


def kernel(
    n_row, n_col,
    pos_ref, obj_ref, probe_ref, amp_ref, mats_ref, perms_ref,
    out_ref,
    pad0, pad1, tot0, tot1, gbuf, probe, amp, mats, perms, amp_p, x_ref, b_ref, t_ref,
    r_in, r_x, r_c, r_d, r_f, r_v,
    local_sem, g_send, g_recv, s_send, s_recv,
):
    i, j = lax.axis_index("row"), lax.axis_index("col")
    core = lax.rem(i, 2)
    c = lax.rem(lax.div(i, 2), 2)
    i_in = i + 1 - 2 * core
    i_x = i - 1 + 2 * core
    j_v = j - 1 + 2 * c
    j_f = j + 1 - 2 * c
    has_x = jnp.logical_and(i_x >= 0, i_x < n_row)
    has_v = jnp.logical_and(j_v >= 0, j_v < n_col)
    has_f = jnp.logical_and(j_f >= 0, j_f < n_col)
    has_d = jnp.logical_and(has_x, has_v)
    ix = jnp.clip(i_x, 0, n_row - 1)
    jv = jnp.clip(j_v, 0, n_col - 1)
    jf = jnp.clip(j_f, 0, n_col - 1)
    always = None
    pads, tots = (pad0, pad1), (tot0, tot1)

    def at(start):
        return pl.ds(pl.multiple_of(start, HALF), HALF)

    x_rows, in_rows = at(HALF * core), at(HALF * (1 - core))
    x_rows_p, in_rows_p = at(MARGIN + HALF * core), at(MARGIN + HALF * (1 - core))

    border = jnp.logical_not(jnp.logical_and(has_x, jnp.logical_and(has_v, has_f)))

    @pl.when(border)
    def _():
        def zero(r):
            for pad in pads:
                pad[:, :, pl.ds(r, ROWS), :] = jnp.zeros((2, 4, ROWS, HALF), jnp.float32)

        rows_loop(WIDE, zero)

    barrier = pltpu.get_barrier_semaphore()

    def when(cond, fn):
        if cond is None:
            fn()
        else:
            pl.when(cond)(fn)

    partners = ((None, (i_in, j)), (has_x, (ix, j)), (has_d, (ix, jv)), (has_v, (i, jv)), (has_f, (i, jf)))
    for cond, dev in partners:
        when(cond, lambda dev=dev: pl.semaphore_signal(barrier, inc=1, device_id=dev, device_id_type=MESH))
    one = lambda cond: cond.astype(jnp.int32)
    pl.semaphore_wait(barrier, 1 + one(has_x) + one(has_d) + one(has_v) + one(has_f))

    def gather(s):
        pad = pads[s]
        dst_x, dst_in = at(3 * HALF * (1 - core)), at(3 * HALF * core)
        f_src, f_dst = at(HALF * (1 - c)), 3 * c
        v_src, v_dst = at(HALF * c), 3 * (1 - c)
        west, east = pl.ds(0, HALF), pl.ds(HALF, HALF)
        obj = obj_ref.at[s]
        table = {
            G_FX: (has_f, has_v, obj.at[:, x_rows, f_src], pad.at[:, f_dst, x_rows_p, :], (i, jf)),
            G_FI: (has_f, has_v, obj.at[:, in_rows, f_src], pad.at[:, f_dst, in_rows_p, :], (i, jf)),
            G_VX: (has_v, has_f, obj.at[:, x_rows, v_src], pad.at[:, v_dst, x_rows_p, :], (i, jv)),
            G_VI: (has_v, has_f, obj.at[:, in_rows, v_src], pad.at[:, v_dst, in_rows_p, :], (i, jv)),
            G_CROSS: (has_x, has_x, obj.at[:, x_rows, west], pad.at[:, 1, dst_x, :], (ix, j)),
            G_CROSS2: (has_x, has_x, obj.at[:, x_rows, east], pad.at[:, 2, dst_x, :], (ix, j)),
            G_DIRECT: (has_d, has_d, obj.at[:, x_rows, v_src], pad.at[:, v_dst, dst_x, :], (ix, jv)),
            G_FWD: (has_x, has_x, pad.at[:, f_dst, x_rows_p, :], pad.at[:, f_dst, dst_x, :], (ix, j)),
            G_IN: (always, always, obj.at[:, in_rows, west], pad.at[:, 1, dst_in, :], (i_in, j)),
            G_IN2: (always, always, obj.at[:, in_rows, east], pad.at[:, 2, dst_in, :], (i_in, j)),
            G_INF: (always, always, pad.at[:, f_dst, in_rows_p, :], pad.at[:, f_dst, dst_in, :], (i_in, j)),
            G_INV: (always, always, pad.at[:, v_dst, in_rows_p, :], pad.at[:, v_dst, dst_in, :], (i_in, j)),
        }
        return {
            k: (sent, comes, pltpu.make_async_remote_copy(
                src_ref=src, dst_ref=dst, send_sem=g_send.at[s, k], recv_sem=g_recv.at[s, k],
                device_id=dev, device_id_type=MESH))
            for k, (sent, comes, src, dst, dev) in table.items()
        }

    def start(copies, *keys):
        for k in keys:
            sent, _, copy = copies[k]
            when(sent, copy.start)

    def arrived(copies, *keys):
        for k in keys:
            _, comes, copy = copies[k]
            when(comes, copy.wait_recv)

    def left(copies, *keys):
        for k in keys:
            sent, _, copy = copies[k]
            when(sent, copy.wait_send)

    g0, g1 = gather(0), gather(1)
    rest = (G_IN, G_IN2, G_CROSS, G_CROSS2, G_FI, G_VI, G_VX, G_DIRECT)
    start(g0, G_FX)
    start(g1, G_FX)
    start(g0, *rest)

    inner = pl.ds(MARGIN, TILE)
    locals_ = [
        pltpu.make_async_copy(obj_ref.at[s, :, :, pl.ds(HALF * k, HALF)], pad.at[:, 1 + k, inner, :], local_sem.at[4 + 2 * s + k])
        for s, pad in enumerate(pads)
        for k in range(2)
    ] + [
        pltpu.make_async_copy(probe_ref, probe, local_sem.at[0]),
        pltpu.make_async_copy(amp_ref, amp, local_sem.at[1]),
        pltpu.make_async_copy(mats_ref, mats, local_sem.at[2]),
        pltpu.make_async_copy(perms_ref, perms, local_sem.at[3]),
    ]
    for copy in locals_:
        copy.start()

    start(g1, *rest)

    def clear(r):
        for w in range(2):
            gbuf[w, :, :, pl.ds(r, ROWS), :] = jnp.zeros((2, 5, ROWS, HALF), jnp.float32)

    rows_loop(3 * TILE, clear)
    for copy in locals_[5:]:
        copy.wait()

    def order(w, carry):
        rest = amp[w]
        total = None
        for _ in range(3):
            piece = rest.astype(jnp.bfloat16)
            rest = rest - piece.astype(jnp.float32)
            part = dot(perms[1], dot(piece, perms[0]).astype(jnp.bfloat16))
            total = part if total is None else total + part
        amp_p[w] = total
        return carry

    lax.fori_loop(0, 2, order, 0)
    for copy in locals_[:5]:
        copy.wait()

    lane = lax.broadcasted_iota(jnp.int32, (ROWS, HALF), 1)

    def place(w):
        y, x = pos_ref[0, 0, w, 0, 0], pos_ref[0, 0, w, 0, 1]
        q = jnp.minimum(lax.div(x, HALF), 1)
        return y, q, x - q * HALF

    def window(pad, w, part, r):
        y, block, s = place(w)
        turn = lax.rem(HALF - s, HALF)
        v = [pltpu.roll(pad[part, block + k, pl.ds(y + r, ROWS), :], turn, 1) for k in range(3)]
        own = lane < HALF - s
        return jnp.concatenate([jnp.where(own, v[0], v[1]), jnp.where(own, v[1], v[2])], 1)

    def finish_gather(copies):
        arrived(copies, G_FI)
        start(copies, G_INF)
        arrived(copies, G_VI)
        start(copies, G_INV)
        arrived(copies, G_VX, G_CROSS, G_CROSS2, G_DIRECT, G_IN, G_IN2, G_FWD, G_INF, G_INV)

    for copies in (g0, g1):
        arrived(copies, G_FX)
        start(copies, G_FWD)
    finish_gather(g0)

    for w in range(2):
        def enter(r, w=w):
            rows = pl.ds(r, ROWS)
            tr, ti = 1.0 + window(pad0, w, 0, r), window(pad0, w, 1, r)
            pr, pi = probe[0, rows, :], probe[1, rows, :]
            x_ref[w, 0, rows, :] = pr * tr - pi * ti
            x_ref[w, 1, rows, :] = pr * ti + pi * tr

        rows_loop(TILE, enter)
    transform(x_ref, b_ref, mats, T_A, True, True)

    finish_gather(g1)

    for w in range(2):
        def leave(r, w=w):
            rows = pl.ds(r, ROWS)
            tr, ti = 1.0 + window(pad1, w, 0, r), window(pad1, w, 1, r)
            t_ref[w, 0, rows, :] = tr
            t_ref[w, 1, rows, :] = ti
            br, bi = b_ref[w, 0, rows, :], b_ref[w, 1, rows, :]
            x_ref[w, 0, rows, :] = br * tr - bi * ti
            x_ref[w, 1, rows, :] = br * ti + bi * tr

        rows_loop(TILE, leave)
    transform(x_ref, x_ref, mats, T_F, True, False)

    for w in range(2):
        def residual(r, w=w):
            rows = pl.ds(r, ROWS)
            fr, fi = x_ref[w, 0, rows, :], x_ref[w, 1, rows, :]
            keep = 1.0 - amp_p[w, rows, :] * lax.rsqrt(fr * fr + fi * fi + 1.0)
            x_ref[w, 0, rows, :] = fr * keep
            x_ref[w, 1, rows, :] = fi * keep

        rows_loop(TILE, residual)
    transform(x_ref, x_ref, mats, T_FI, False, True)

    def turned(w, part, r, v):
        _, _, s = place(w)
        turn = lax.rem(s, HALF)
        a, b = (pltpu.roll(v[:, HALF * k : HALF * (k + 1)], turn, 1) for k in range(2))
        own = lane >= s
        rows = pl.ds(TILE + r, ROWS)
        gbuf[w, part, 1, rows, :] = jnp.where(own, a, 0.0)
        gbuf[w, part, 2, rows, :] = jnp.where(own, b, a)
        gbuf[w, part, 3, rows, :] = jnp.where(own, 0.0, b)

    def add_up(tot):
        def chunk(r):
            for part in range(2):
                for k in range(4):
                    total = None
                    for w in range(2):
                        y, block, _ = place(w)
                        v = gbuf[w, part, 1 - block + k, pl.ds(TILE - y + r, ROWS), :]
                        total = v if total is None else total + v
                    tot[part, k, pl.ds(r, ROWS), :] = total

        rows_loop(WIDE, chunk)

    def scatter(s):
        tot = tots[s]
        cross_rows, inner_rows = at(3 * HALF * core), at(3 * HALF * (1 - core))
        f_blk, v_blk = 3 * (1 - c), 3 * c
        table = {
            S_CORNER: (has_x, has_x, tot.at[:, f_blk, cross_rows, :], r_c.at[s], (ix, j)),
            S_CROSS: (has_x, has_x, tot.at[:, pl.ds(1, 2), cross_rows, :], r_x.at[s], (ix, j)),
            S_DIRECT: (has_d, has_d, tot.at[:, v_blk, cross_rows, :], r_d.at[s], (ix, jv)),
            S_IN: (always, always, tot.at[:, :, inner_rows, :], r_in.at[s], (i_in, j)),
            S_FX: (has_f, has_v, tot.at[:, f_blk, x_rows_p, :], r_f.at[s, :, x_rows, :], (i, jf)),
            S_FI: (has_f, has_v, tot.at[:, f_blk, in_rows_p, :], r_f.at[s, :, in_rows, :], (i, jf)),
            S_VX: (has_v, has_f, tot.at[:, v_blk, x_rows_p, :], r_v.at[s, :, x_rows, :], (i, jv)),
            S_VI: (has_v, has_f, tot.at[:, v_blk, in_rows_p, :], r_v.at[s, :, in_rows, :], (i, jv)),
        }
        return {
            k: (sent, comes, pltpu.make_async_remote_copy(
                src_ref=src, dst_ref=dst, send_sem=s_send.at[s, k], recv_sem=s_recv.at[s, k],
                device_id=dev, device_id_type=MESH))
            for k, (sent, comes, src, dst, dev) in table.items()
        }

    def add_in(s):
        tot = tots[s]

        def chunk(r):
            rows = pl.ds(pl.multiple_of(MARGIN + HALF * (1 - core) + r, ROWS), ROWS)
            tot[:, :, rows, :] = tot[:, :, rows, :] + r_in[s, :, :, pl.ds(r, ROWS), :]

        rows_loop(HALF, chunk)

    def add_corner(s):
        tot = tots[s]

        def chunk(r):
            rows = pl.ds(pl.multiple_of(MARGIN + HALF * core + r, ROWS), ROWS)
            tot[:, 3 * c, rows, :] = tot[:, 3 * c, rows, :] + r_c[s, :, pl.ds(r, ROWS), :]

        @pl.when(has_x)
        def _():
            rows_loop(HALF, chunk)

    def send_early(s, copies):
        start(copies, S_CORNER, S_IN, S_FX, S_CROSS, S_DIRECT)

    def send_inner(s, copies):
        arrived(copies, S_IN)
        add_in(s)
        start(copies, S_FI, S_VI)

    def send_late(s, copies):
        arrived(copies, S_CORNER)
        add_corner(s)
        start(copies, S_VX)

    def own_part(s):
        def chunk(r):
            rows, rows_p = pl.ds(r, ROWS), pl.ds(MARGIN + r, ROWS)
            for k in range(2):
                cols = slice(HALF * k, HALF * (k + 1))
                out_ref[s, :, rows, cols] = pads[s][:, 1 + k, rows_p, :] - STEP * tots[s][:, 1 + k, rows_p, :]

        rows_loop(TILE, chunk)

    def take(s, copies, key, cond, rows0, cols, part):
        if key is not None:
            arrived(copies, key)

        def chunk(r):
            rows = pl.ds(pl.multiple_of(rows0 + r, ROWS), ROWS)
            out_ref[s, :, rows, cols] = out_ref[s, :, rows, cols] - STEP * part(r)

        @pl.when(cond)
        def _():
            rows_loop(HALF, chunk)

    def finish(s, copies):
        x0, in0 = HALF * core, HALF * (1 - core)
        f_cols, v_cols = at(HALF * c), at(HALF * (1 - c))
        west, east = slice(0, HALF), slice(HALF, TILE)
        take(s, copies, S_DIRECT, has_d, x0, f_cols, lambda r: r_d[s, :, pl.ds(r, ROWS), :])
        take(s, copies, S_CROSS, has_x, x0, west, lambda r: r_x[s, :, 0, pl.ds(r, ROWS), :])
        take(s, copies, None, has_x, x0, east, lambda r: r_x[s, :, 1, pl.ds(r, ROWS), :])
        take(s, copies, S_FX, has_v, x0, f_cols, lambda r: r_f[s, :, pl.ds(pl.multiple_of(x0 + r, ROWS), ROWS), :])
        take(s, copies, S_FI, has_v, in0, f_cols, lambda r: r_f[s, :, pl.ds(pl.multiple_of(in0 + r, ROWS), ROWS), :])
        take(s, copies, S_VI, has_f, in0, v_cols, lambda r: r_v[s, :, pl.ds(pl.multiple_of(in0 + r, ROWS), ROWS), :])
        take(s, copies, S_VX, has_f, x0, v_cols, lambda r: r_v[s, :, pl.ds(pl.multiple_of(x0 + r, ROWS), ROWS), :])

    for w in range(2):
        def second(r, w=w):
            rows = pl.ds(r, ROWS)
            br, bi = b_ref[w, 0, rows, :], b_ref[w, 1, rows, :]
            cr, ci = x_ref[w, 0, rows, :], x_ref[w, 1, rows, :]
            turned(w, 0, r, br * cr + bi * ci)
            turned(w, 1, r, br * ci - bi * cr)

        rows_loop(TILE, second)
    add_up(tot1)
    s1 = scatter(1)
    send_early(1, s1)

    for w in range(2):
        def back(r, w=w):
            rows = pl.ds(r, ROWS)
            tr, ti = t_ref[w, 0, rows, :], t_ref[w, 1, rows, :]
            cr, ci = x_ref[w, 0, rows, :], x_ref[w, 1, rows, :]
            x_ref[w, 0, rows, :] = tr * cr + ti * ci
            x_ref[w, 1, rows, :] = tr * ci - ti * cr

        rows_loop(TILE, back)
    send_inner(1, s1)
    send_late(1, s1)
    transform(x_ref, x_ref, mats, T_AC, True, True)
    for w in range(2):
        def first_slice(r, w=w):
            rows = pl.ds(r, ROWS)
            pr, pi = probe[0, rows, :], probe[1, rows, :]
            cr, ci = x_ref[w, 0, rows, :], x_ref[w, 1, rows, :]
            turned(w, 0, r, pr * cr + pi * ci)
            turned(w, 1, r, pr * ci - pi * cr)

        rows_loop(TILE, first_slice)
    add_up(tot0)
    s0 = scatter(0)
    send_early(0, s0)
    send_inner(0, s0)
    send_late(0, s0)
    own_part(1)
    own_part(0)
    finish(1, s1)
    finish(0, s0)
    for copies in (g0, g1, s0, s1):
        left(copies, *copies)


def body(n_row, n_col, mats, perms, obj, probe, amplitude, positions):
    any_space = pl.BlockSpec(memory_space=pltpu.HBM)
    vmem = pl.BlockSpec(memory_space=pltpu.VMEM)
    smem = pl.BlockSpec(memory_space=pltpu.SMEM)
    f32 = jnp.float32
    wide = pltpu.VMEM((2, 4, WIDE, HALF), f32)
    field = pltpu.VMEM((2, 2, TILE, TILE), f32)
    return pl.pallas_call(
        functools.partial(kernel, n_row, n_col),
        out_shape=pltpu.VMEM((2, 2, TILE, TILE), f32),
        in_specs=[smem] + [any_space] * 5,
        out_specs=vmem,
        scratch_shapes=[
            wide, wide, wide, wide,
            pltpu.VMEM((2, 2, 5, 3 * TILE, HALF), f32),
            pltpu.VMEM((2, TILE, TILE), f32),
            pltpu.VMEM((2, TILE, TILE), f32),
            pltpu.VMEM(mats.shape, jnp.bfloat16),
            pltpu.VMEM(perms.shape, jnp.bfloat16),
            pltpu.VMEM((2, TILE, TILE), f32),
            field, field, field,
            pltpu.VMEM((2, 2, 4, HALF, HALF), f32),
            pltpu.VMEM((2, 2, 2, HALF, HALF), f32),
            pltpu.VMEM((2, 2, HALF, HALF), f32),
            pltpu.VMEM((2, 2, HALF, HALF), f32),
            pltpu.VMEM((2, 2, TILE, HALF), f32),
            pltpu.VMEM((2, 2, TILE, HALF), f32),
            pltpu.SemaphoreType.DMA((8,)),
            pltpu.SemaphoreType.DMA((2, 12)),
            pltpu.SemaphoreType.DMA((2, 12)),
            pltpu.SemaphoreType.DMA((2, 8)),
            pltpu.SemaphoreType.DMA((2, 8)),
        ],
        compiler_params=pltpu.CompilerParams(
            collective_id=0, has_side_effects=True, vmem_limit_bytes=54 * 1024 * 1024
        ),
        cost_estimate=pl.CostEstimate(flops=3 * 10**9, bytes_accessed=8 * 10**6, transcendentals=131072),
    )(positions, obj, probe, amplitude.reshape(2, TILE, TILE), mats, perms)


def solution(mesh):
    mats, perms = constants()
    mats, perms = jnp.asarray(mats), jnp.asarray(perms)
    placed = (
        P(None, None, "row", "col"),
        P(),
        P("row", "col", None, None, None, None),
        P("row", "col", None, None, None),
    )
    return jax.shard_map(
        functools.partial(body, mesh.shape["row"], mesh.shape["col"], mats, perms),
        mesh=mesh, in_specs=placed, out_specs=P(None, None, "row", "col"), check_vma=False,
    )
```

```python
import functools
import math

import jax
import jax.numpy as jnp
import numpy as np
from jax import lax
from jax.experimental import pallas as pl
from jax.experimental.pallas import tpu as pltpu
from jax.sharding import PartitionSpec as P

TILE = 256
MARGIN = 128
HALF = 128
WIDE = 512
STEP = 0.5
MESH = pl.DeviceIdType.MESH

G_FX, G_FI, G_VX, G_VI, G_CROSS, G_CROSS2, G_DIRECT, G_FWD, G_IN, G_IN2, G_INF, G_INV = range(12)
S_CORNER, S_CROSS, S_DIRECT, S_IN, S_FX, S_FI, S_VX, S_VI = range(8)

T_A, T_F, T_FI, T_AC = range(4)


def real_form(m):
    return np.block([[m.real, m.imag], [-m.imag, m.real]])


def matrices():
    n = np.arange(TILE)
    f = np.where(n < TILE // 2, n, n - TILE)
    h = np.exp(-1j * math.pi * ((f * f) % (4 * TILE)) / (2 * TILE))
    dft = np.exp(-2j * math.pi * ((n[:, None] * n[None, :]) % TILE) / TILE) / math.sqrt(TILE)
    spread = np.conj(dft) @ (h[:, None] * dft)
    c0, c1 = spread[:HALF, :HALF], spread[:HALF, HALF:]
    a = [(c0 + c1) / 2, (c0 - c1) / 2]
    fwd = [dft[:HALF, 0::2], dft[:HALF, 1::2]]
    inv = [np.conj(m.T) for m in fwd]
    ac = [np.conj(m) for m in a]
    return np.stack([np.stack([real_form(m) for m in pair]) for pair in (a, fwd, inv, ac)])


def constants():
    right = matrices()
    both = np.stack([right, np.swapaxes(right, -1, -2)], 2)
    both = both.astype(np.float32)
    high = both.astype(jnp.bfloat16)
    low = (both - high.astype(np.float32)).astype(jnp.bfloat16)
    mats = np.stack([high, low], 3)
    order = np.concatenate([np.arange(0, TILE, 2), np.arange(1, TILE, 2)])
    perm = np.zeros((TILE, TILE), np.float32)
    perm[order, np.arange(TILE)] = 1.0
    perms = np.stack([perm, perm.T]).astype(jnp.bfloat16)
    return mats, perms


def split(x):
    high = x.astype(jnp.bfloat16)
    low = (x - high.astype(jnp.float32)).astype(jnp.bfloat16)
    return high, low


def dot(a, b):
    return jnp.dot(a, b, preferred_element_type=jnp.float32)


def mm_right(x, high, low):
    xh, xl = split(x)
    return dot(xh, high) + (dot(xl, high) + dot(xh, low))


def mm_left(high, low, x):
    xh, xl = split(x)
    return dot(high, xh) + (dot(high, xl) + dot(low, xh))


def transform(src, dst, mats, which, pre, post):
    def one(w, carry):
        xr, xi = src[w, 0], src[w, 1]
        r0, r1, i0, i1 = xr[:, :HALF], xr[:, HALF:], xi[:, :HALF], xi[:, HALF:]
        if pre:
            r0, r1, i0, i1 = r0 + r1, r0 - r1, i0 + i1, i0 - i1
        ys = mm_right(jnp.concatenate([r0, i0], 1), mats[which, 0, 0, 0], mats[which, 0, 0, 1])
        yd = mm_right(jnp.concatenate([r1, i1], 1), mats[which, 1, 0, 0], mats[which, 1, 0, 1])
        if post:
            ys, yd = ys + yd, ys - yd
        yr = jnp.concatenate([ys[:, :HALF], yd[:, :HALF]], 1)
        yi = jnp.concatenate([ys[:, HALF:], yd[:, HALF:]], 1)
        r0, r1, i0, i1 = yr[:HALF], yr[HALF:], yi[:HALF], yi[HALF:]
        if pre:
            r0, r1, i0, i1 = r0 + r1, r0 - r1, i0 + i1, i0 - i1
        zs = mm_left(mats[which, 0, 1, 0], mats[which, 0, 1, 1], jnp.concatenate([r0, i0], 0))
        zd = mm_left(mats[which, 1, 1, 0], mats[which, 1, 1, 1], jnp.concatenate([r1, i1], 0))
        if post:
            zs, zd = zs + zd, zs - zd
        dst[w, 0, :HALF, :] = zs[:HALF]
        dst[w, 0, HALF:, :] = zd[:HALF]
        dst[w, 1, :HALF, :] = zs[HALF:]
        dst[w, 1, HALF:, :] = zd[HALF:]
        return carry

    lax.fori_loop(0, 2, one, 0, unroll=True)


ROWS = 32


def rows_loop(count, fn):
    def step(k, carry):
        fn(pl.multiple_of(k * ROWS, ROWS))
        return carry

    lax.fori_loop(0, count // ROWS, step, 0, unroll=4)


def kernel(
    n_row, n_col,
    pos_ref, obj_ref, probe_ref, amp_ref, mats_ref, perms_ref,
    out_ref,
    pad0, pad1, tot0, tot1, gbuf, probe, amp, mats, perms, amp_p, x_ref, b_ref, t_ref,
    r_in, r_x, r_c, r_d, r_f, r_v,
    local_sem, g_send, g_recv, s_send, s_recv,
):
    i, j = lax.axis_index("row"), lax.axis_index("col")
    core = lax.rem(i, 2)
    c = lax.rem(lax.div(i, 2), 2)
    i_in = i + 1 - 2 * core
    i_x = i - 1 + 2 * core
    j_v = j - 1 + 2 * c
    j_f = j + 1 - 2 * c
    has_x = jnp.logical_and(i_x >= 0, i_x < n_row)
    has_v = jnp.logical_and(j_v >= 0, j_v < n_col)
    has_f = jnp.logical_and(j_f >= 0, j_f < n_col)
    has_d = jnp.logical_and(has_x, has_v)
    ix = jnp.clip(i_x, 0, n_row - 1)
    jv = jnp.clip(j_v, 0, n_col - 1)
    jf = jnp.clip(j_f, 0, n_col - 1)
    always = None
    pads, tots = (pad0, pad1), (tot0, tot1)

    def at(start):
        return pl.ds(pl.multiple_of(start, HALF), HALF)

    x_rows, in_rows = at(HALF * core), at(HALF * (1 - core))
    x_rows_p, in_rows_p = at(MARGIN + HALF * core), at(MARGIN + HALF * (1 - core))

    border = jnp.logical_not(jnp.logical_and(has_x, jnp.logical_and(has_v, has_f)))

    @pl.when(border)
    def _():
        def zero(r):
            for pad in pads:
                pad[:, :, pl.ds(r, ROWS), :] = jnp.zeros((2, 4, ROWS, HALF), jnp.float32)

        rows_loop(WIDE, zero)

    barrier = pltpu.get_barrier_semaphore()

    def when(cond, fn):
        if cond is None:
            fn()
        else:
            pl.when(cond)(fn)

    partners = ((None, (i_in, j)), (has_x, (ix, j)), (has_d, (ix, jv)), (has_v, (i, jv)), (has_f, (i, jf)))
    for cond, dev in partners:
        when(cond, lambda dev=dev: pl.semaphore_signal(barrier, inc=1, device_id=dev, device_id_type=MESH))
    one = lambda cond: cond.astype(jnp.int32)
    pl.semaphore_wait(barrier, 1 + one(has_x) + one(has_d) + one(has_v) + one(has_f))

    def gather(s):
        pad = pads[s]
        dst_x, dst_in = at(3 * HALF * (1 - core)), at(3 * HALF * core)
        f_src, f_dst = at(HALF * (1 - c)), 3 * c
        v_src, v_dst = at(HALF * c), 3 * (1 - c)
        west, east = pl.ds(0, HALF), pl.ds(HALF, HALF)
        obj = obj_ref.at[s]
        table = {
            G_FX: (has_f, has_v, obj.at[:, x_rows, f_src], pad.at[:, f_dst, x_rows_p, :], (i, jf)),
            G_FI: (has_f, has_v, obj.at[:, in_rows, f_src], pad.at[:, f_dst, in_rows_p, :], (i, jf)),
            G_VX: (has_v, has_f, obj.at[:, x_rows, v_src], pad.at[:, v_dst, x_rows_p, :], (i, jv)),
            G_VI: (has_v, has_f, obj.at[:, in_rows, v_src], pad.at[:, v_dst, in_rows_p, :], (i, jv)),
            G_CROSS: (has_x, has_x, obj.at[:, x_rows, west], pad.at[:, 1, dst_x, :], (ix, j)),
            G_CROSS2: (has_x, has_x, obj.at[:, x_rows, east], pad.at[:, 2, dst_x, :], (ix, j)),
            G_DIRECT: (has_d, has_d, obj.at[:, x_rows, v_src], pad.at[:, v_dst, dst_x, :], (ix, jv)),
            G_FWD: (has_x, has_x, pad.at[:, f_dst, x_rows_p, :], pad.at[:, f_dst, dst_x, :], (ix, j)),
            G_IN: (always, always, obj.at[:, in_rows, west], pad.at[:, 1, dst_in, :], (i_in, j)),
            G_IN2: (always, always, obj.at[:, in_rows, east], pad.at[:, 2, dst_in, :], (i_in, j)),
            G_INF: (always, always, pad.at[:, f_dst, in_rows_p, :], pad.at[:, f_dst, dst_in, :], (i_in, j)),
            G_INV: (always, always, pad.at[:, v_dst, in_rows_p, :], pad.at[:, v_dst, dst_in, :], (i_in, j)),
        }
        return {
            k: (sent, comes, pltpu.make_async_remote_copy(
                src_ref=src, dst_ref=dst, send_sem=g_send.at[s, k], recv_sem=g_recv.at[s, k],
                device_id=dev, device_id_type=MESH))
            for k, (sent, comes, src, dst, dev) in table.items()
        }

    def start(copies, *keys):
        for k in keys:
            sent, _, copy = copies[k]
            when(sent, copy.start)

    def arrived(copies, *keys):
        for k in keys:
            _, comes, copy = copies[k]
            when(comes, copy.wait_recv)

    def left(copies, *keys):
        for k in keys:
            sent, _, copy = copies[k]
            when(sent, copy.wait_send)

    g0, g1 = gather(0), gather(1)
    inner_first = (G_FI, G_VI, G_IN, G_IN2)
    then = (G_CROSS, G_CROSS2, G_VX, G_DIRECT)
    start(g0, G_FX)
    start(g1, G_FX)
    start(g0, *inner_first, *then)

    inner = pl.ds(MARGIN, TILE)
    locals_ = [
        pltpu.make_async_copy(obj_ref.at[s, :, :, pl.ds(HALF * k, HALF)], pad.at[:, 1 + k, inner, :], local_sem.at[4 + 2 * s + k])
        for s, pad in enumerate(pads)
        for k in range(2)
    ] + [
        pltpu.make_async_copy(probe_ref, probe, local_sem.at[0]),
        pltpu.make_async_copy(amp_ref, amp, local_sem.at[1]),
        pltpu.make_async_copy(mats_ref, mats, local_sem.at[2]),
        pltpu.make_async_copy(perms_ref, perms, local_sem.at[3]),
    ]
    for copy in locals_:
        copy.start()

    start(g1, *inner_first)

    def clear(r):
        for w in range(2):
            gbuf[w, :, :, pl.ds(r, ROWS), :] = jnp.zeros((2, 5, ROWS, HALF), jnp.float32)

    rows_loop(3 * TILE, clear)
    for copy in locals_[5:]:
        copy.wait()

    def order(w, carry):
        rest = amp[w]
        total = None
        for _ in range(3):
            piece = rest.astype(jnp.bfloat16)
            rest = rest - piece.astype(jnp.float32)
            part = dot(perms[1], dot(piece, perms[0]).astype(jnp.bfloat16))
            total = part if total is None else total + part
        amp_p[w] = total
        return carry

    lax.fori_loop(0, 2, order, 0)
    for copy in locals_[:5]:
        copy.wait()

    lane = lax.broadcasted_iota(jnp.int32, (ROWS, HALF), 1)

    def place(w):
        y, x = pos_ref[0, 0, w, 0, 0], pos_ref[0, 0, w, 0, 1]
        q = jnp.minimum(lax.div(x, HALF), 1)
        return y, q, x - q * HALF

    def window(pad, w, part, r):
        y, block, s = place(w)
        turn = lax.rem(HALF - s, HALF)
        v = [pltpu.roll(pad[part, block + k, pl.ds(y + r, ROWS), :], turn, 1) for k in range(3)]
        own = lane < HALF - s
        return jnp.concatenate([jnp.where(own, v[0], v[1]), jnp.where(own, v[1], v[2])], 1)

    def finish_gather(copies):
        arrived(copies, G_FI)
        start(copies, G_INF)
        arrived(copies, G_VI)
        start(copies, G_INV)
        arrived(copies, G_VX, G_CROSS, G_CROSS2, G_DIRECT, G_IN, G_IN2, G_FWD, G_INF, G_INV)

    for copies in (g0, g1):
        arrived(copies, G_FX)
        start(copies, G_FWD)
    finish_gather(g0)
    start(g1, *then)

    for w in range(2):
        def enter(r, w=w):
            rows = pl.ds(r, ROWS)
            tr, ti = 1.0 + window(pad0, w, 0, r), window(pad0, w, 1, r)
            pr, pi = probe[0, rows, :], probe[1, rows, :]
            x_ref[w, 0, rows, :] = pr * tr - pi * ti
            x_ref[w, 1, rows, :] = pr * ti + pi * tr

        rows_loop(TILE, enter)
    transform(x_ref, b_ref, mats, T_A, True, True)

    finish_gather(g1)

    for w in range(2):
        def leave(r, w=w):
            rows = pl.ds(r, ROWS)
            tr, ti = 1.0 + window(pad1, w, 0, r), window(pad1, w, 1, r)
            t_ref[w, 0, rows, :] = tr
            t_ref[w, 1, rows, :] = ti
            br, bi = b_ref[w, 0, rows, :], b_ref[w, 1, rows, :]
            x_ref[w, 0, rows, :] = br * tr - bi * ti
            x_ref[w, 1, rows, :] = br * ti + bi * tr

        rows_loop(TILE, leave)
    transform(x_ref, x_ref, mats, T_F, True, False)

    for w in range(2):
        def residual(r, w=w):
            rows = pl.ds(r, ROWS)
            fr, fi = x_ref[w, 0, rows, :], x_ref[w, 1, rows, :]
            keep = 1.0 - amp_p[w, rows, :] * lax.rsqrt(fr * fr + fi * fi + 1.0)
            x_ref[w, 0, rows, :] = fr * keep
            x_ref[w, 1, rows, :] = fi * keep

        rows_loop(TILE, residual)
    transform(x_ref, x_ref, mats, T_FI, False, True)

    def turned(w, part, r, v):
        _, _, s = place(w)
        turn = lax.rem(s, HALF)
        a, b = (pltpu.roll(v[:, HALF * k : HALF * (k + 1)], turn, 1) for k in range(2))
        own = lane >= s
        rows = pl.ds(TILE + r, ROWS)
        gbuf[w, part, 1, rows, :] = jnp.where(own, a, 0.0)
        gbuf[w, part, 2, rows, :] = jnp.where(own, b, a)
        gbuf[w, part, 3, rows, :] = jnp.where(own, 0.0, b)

    def add_up(tot, row0, count, blocks):
        def chunk(r):
            r = pl.multiple_of(row0 + r, ROWS)
            for part in range(2):
                for k in blocks:
                    total = None
                    for w in range(2):
                        y, block, _ = place(w)
                        v = gbuf[w, part, 1 - block + k, pl.ds(TILE - y + r, ROWS), :]
                        total = v if total is None else total + v
                    tot[part, k, pl.ds(r, ROWS), :] = total

        rows_loop(count, chunk)

    def scatter(s):
        tot = tots[s]
        cross_rows, inner_rows = at(3 * HALF * core), at(3 * HALF * (1 - core))
        f_blk, v_blk = 3 * (1 - c), 3 * c
        table = {
            S_CORNER: (has_x, has_x, tot.at[:, f_blk, cross_rows, :], r_c.at[s], (ix, j)),
            S_CROSS: (has_x, has_x, tot.at[:, pl.ds(1, 2), cross_rows, :], r_x.at[s], (ix, j)),
            S_DIRECT: (has_d, has_d, tot.at[:, v_blk, cross_rows, :], r_d.at[s], (ix, jv)),
            S_IN: (always, always, tot.at[:, :, inner_rows, :], r_in.at[s], (i_in, j)),
            S_FX: (has_f, has_v, tot.at[:, f_blk, x_rows_p, :], r_f.at[s, :, x_rows, :], (i, jf)),
            S_FI: (has_f, has_v, tot.at[:, f_blk, in_rows_p, :], r_f.at[s, :, in_rows, :], (i, jf)),
            S_VX: (has_v, has_f, tot.at[:, v_blk, x_rows_p, :], r_v.at[s, :, x_rows, :], (i, jv)),
            S_VI: (has_v, has_f, tot.at[:, v_blk, in_rows_p, :], r_v.at[s, :, in_rows, :], (i, jv)),
        }
        return {
            k: (sent, comes, pltpu.make_async_remote_copy(
                src_ref=src, dst_ref=dst, send_sem=s_send.at[s, k], recv_sem=s_recv.at[s, k],
                device_id=dev, device_id_type=MESH))
            for k, (sent, comes, src, dst, dev) in table.items()
        }

    def add_in(s):
        tot = tots[s]

        def chunk(r):
            rows = pl.ds(pl.multiple_of(MARGIN + HALF * (1 - core) + r, ROWS), ROWS)
            tot[:, :, rows, :] = tot[:, :, rows, :] + r_in[s, :, :, pl.ds(r, ROWS), :]

        rows_loop(HALF, chunk)

    def add_corner(s):
        tot = tots[s]

        def chunk(r):
            rows = pl.ds(pl.multiple_of(MARGIN + HALF * core + r, ROWS), ROWS)
            tot[:, 3 * c, rows, :] = tot[:, 3 * c, rows, :] + r_c[s, :, pl.ds(r, ROWS), :]

        @pl.when(has_x)
        def _():
            rows_loop(HALF, chunk)

    def send_early(s, copies):
        everywhere = range(4)
        add_up(tots[s], 3 * HALF * core, HALF, everywhere)
        start(copies, S_CORNER, S_CROSS, S_DIRECT)
        add_up(tots[s], MARGIN, TILE, (0, 3))
        start(copies, S_FX)
        add_up(tots[s], 3 * HALF * (1 - core), HALF, everywhere)
        start(copies, S_IN)
        add_up(tots[s], MARGIN, TILE, (1, 2))

    def send_inner(s, copies):
        arrived(copies, S_IN)
        add_in(s)
        start(copies, S_FI, S_VI)

    def send_late(s, copies):
        arrived(copies, S_CORNER)
        add_corner(s)
        start(copies, S_VX)

    def own_part(s):
        def chunk(r):
            rows, rows_p = pl.ds(r, ROWS), pl.ds(MARGIN + r, ROWS)
            for k in range(2):
                cols = slice(HALF * k, HALF * (k + 1))
                out_ref[s, :, rows, cols] = pads[s][:, 1 + k, rows_p, :] - STEP * tots[s][:, 1 + k, rows_p, :]

        rows_loop(TILE, chunk)

    def take(s, copies, key, cond, rows0, cols, part):
        if key is not None:
            arrived(copies, key)

        def chunk(r):
            rows = pl.ds(pl.multiple_of(rows0 + r, ROWS), ROWS)
            out_ref[s, :, rows, cols] = out_ref[s, :, rows, cols] - STEP * part(r)

        @pl.when(cond)
        def _():
            rows_loop(HALF, chunk)

    def finish(s, copies):
        x0, in0 = HALF * core, HALF * (1 - core)
        f_cols, v_cols = at(HALF * c), at(HALF * (1 - c))
        west, east = slice(0, HALF), slice(HALF, TILE)
        take(s, copies, S_DIRECT, has_d, x0, f_cols, lambda r: r_d[s, :, pl.ds(r, ROWS), :])
        take(s, copies, S_CROSS, has_x, x0, west, lambda r: r_x[s, :, 0, pl.ds(r, ROWS), :])
        take(s, copies, None, has_x, x0, east, lambda r: r_x[s, :, 1, pl.ds(r, ROWS), :])
        take(s, copies, S_FX, has_v, x0, f_cols, lambda r: r_f[s, :, pl.ds(pl.multiple_of(x0 + r, ROWS), ROWS), :])
        take(s, copies, S_FI, has_v, in0, f_cols, lambda r: r_f[s, :, pl.ds(pl.multiple_of(in0 + r, ROWS), ROWS), :])
        take(s, copies, S_VI, has_f, in0, v_cols, lambda r: r_v[s, :, pl.ds(pl.multiple_of(in0 + r, ROWS), ROWS), :])
        take(s, copies, S_VX, has_f, x0, v_cols, lambda r: r_v[s, :, pl.ds(pl.multiple_of(x0 + r, ROWS), ROWS), :])

    for w in range(2):
        def second(r, w=w):
            rows = pl.ds(r, ROWS)
            br, bi = b_ref[w, 0, rows, :], b_ref[w, 1, rows, :]
            cr, ci = x_ref[w, 0, rows, :], x_ref[w, 1, rows, :]
            turned(w, 0, r, br * cr + bi * ci)
            turned(w, 1, r, br * ci - bi * cr)

        rows_loop(TILE, second)
    s1 = scatter(1)
    send_early(1, s1)

    for w in range(2):
        def back(r, w=w):
            rows = pl.ds(r, ROWS)
            tr, ti = t_ref[w, 0, rows, :], t_ref[w, 1, rows, :]
            cr, ci = x_ref[w, 0, rows, :], x_ref[w, 1, rows, :]
            x_ref[w, 0, rows, :] = tr * cr + ti * ci
            x_ref[w, 1, rows, :] = tr * ci - ti * cr

        rows_loop(TILE, back)
    send_inner(1, s1)
    send_late(1, s1)
    transform(x_ref, x_ref, mats, T_AC, True, True)
    for w in range(2):
        def first_slice(r, w=w):
            rows = pl.ds(r, ROWS)
            pr, pi = probe[0, rows, :], probe[1, rows, :]
            cr, ci = x_ref[w, 0, rows, :], x_ref[w, 1, rows, :]
            turned(w, 0, r, pr * cr + pi * ci)
            turned(w, 1, r, pr * ci - pi * cr)

        rows_loop(TILE, first_slice)
    s0 = scatter(0)
    send_early(0, s0)
    send_inner(0, s0)
    send_late(0, s0)
    own_part(1)
    own_part(0)
    finish(1, s1)
    finish(0, s0)
    for copies in (g0, g1, s0, s1):
        left(copies, *copies)


def body(n_row, n_col, mats, perms, obj, probe, amplitude, positions):
    any_space = pl.BlockSpec(memory_space=pltpu.HBM)
    vmem = pl.BlockSpec(memory_space=pltpu.VMEM)
    smem = pl.BlockSpec(memory_space=pltpu.SMEM)
    f32 = jnp.float32
    wide = pltpu.VMEM((2, 4, WIDE, HALF), f32)
    field = pltpu.VMEM((2, 2, TILE, TILE), f32)
    return pl.pallas_call(
        functools.partial(kernel, n_row, n_col),
        out_shape=pltpu.VMEM((2, 2, TILE, TILE), f32),
        in_specs=[smem] + [any_space] * 5,
        out_specs=vmem,
        scratch_shapes=[
            wide, wide, wide, wide,
            pltpu.VMEM((2, 2, 5, 3 * TILE, HALF), f32),
            pltpu.VMEM((2, TILE, TILE), f32),
            pltpu.VMEM((2, TILE, TILE), f32),
            pltpu.VMEM(mats.shape, jnp.bfloat16),
            pltpu.VMEM(perms.shape, jnp.bfloat16),
            pltpu.VMEM((2, TILE, TILE), f32),
            field, field, field,
            pltpu.VMEM((2, 2, 4, HALF, HALF), f32),
            pltpu.VMEM((2, 2, 2, HALF, HALF), f32),
            pltpu.VMEM((2, 2, HALF, HALF), f32),
            pltpu.VMEM((2, 2, HALF, HALF), f32),
            pltpu.VMEM((2, 2, TILE, HALF), f32),
            pltpu.VMEM((2, 2, TILE, HALF), f32),
            pltpu.SemaphoreType.DMA((8,)),
            pltpu.SemaphoreType.DMA((2, 12)),
            pltpu.SemaphoreType.DMA((2, 12)),
            pltpu.SemaphoreType.DMA((2, 8)),
            pltpu.SemaphoreType.DMA((2, 8)),
        ],
        compiler_params=pltpu.CompilerParams(
            collective_id=0, has_side_effects=True, vmem_limit_bytes=54 * 1024 * 1024
        ),
        cost_estimate=pl.CostEstimate(flops=3 * 10**9, bytes_accessed=8 * 10**6, transcendentals=131072),
    )(positions, obj, probe, amplitude.reshape(2, TILE, TILE), mats, perms)


def solution(mesh):
    mats, perms = constants()
    mats, perms = jnp.asarray(mats), jnp.asarray(perms)
    placed = (
        P(None, None, "row", "col"),
        P(),
        P("row", "col", None, None, None, None),
        P("row", "col", None, None, None),
    )
    return jax.shard_map(
        functools.partial(body, mesh.shape["row"], mesh.shape["col"], mats, perms),
        mesh=mesh, in_specs=placed, out_specs=P(None, None, "row", "col"), check_vma=False,
    )
```

```python
import functools
import math

import jax
import jax.numpy as jnp
import numpy as np
from jax import lax
from jax.experimental import pallas as pl
from jax.experimental.pallas import tpu as pltpu
from jax.sharding import PartitionSpec as P

TILE = 256
MARGIN = 128
HALF = 128
WIDE = 512
STEP = 0.5
MESH = pl.DeviceIdType.MESH

G_FX, G_FI, G_VX, G_VI, G_CROSS, G_CROSS2, G_DIRECT, G_FWD, G_IN, G_IN2, G_INF, G_INV = range(12)
S_CORNER, S_CROSS, S_DIRECT, S_IN, S_FX, S_FI, S_VX, S_VI = range(8)

T_A, T_F, T_FI, T_AC = range(4)


def real_form(m):
    return np.block([[m.real, m.imag], [-m.imag, m.real]])


def matrices():
    n = np.arange(TILE)
    f = np.where(n < TILE // 2, n, n - TILE)
    h = np.exp(-1j * math.pi * ((f * f) % (4 * TILE)) / (2 * TILE))
    dft = np.exp(-2j * math.pi * ((n[:, None] * n[None, :]) % TILE) / TILE) / math.sqrt(TILE)
    spread = np.conj(dft) @ (h[:, None] * dft)
    c0, c1 = spread[:HALF, :HALF], spread[:HALF, HALF:]
    a = [(c0 + c1) / 2, (c0 - c1) / 2]
    fwd = [dft[:HALF, 0::2], dft[:HALF, 1::2]]
    inv = [np.conj(m.T) for m in fwd]
    ac = [np.conj(m) for m in a]
    return np.stack([np.stack([real_form(m) for m in pair]) for pair in (a, fwd, inv, ac)])


def constants():
    right = matrices()
    both = np.stack([right, np.swapaxes(right, -1, -2)], 2)
    both = both.astype(np.float32)
    high = both.astype(jnp.bfloat16)
    low = (both - high.astype(np.float32)).astype(jnp.bfloat16)
    mats = np.stack([high, low], 3)
    order = np.concatenate([np.arange(0, TILE, 2), np.arange(1, TILE, 2)])
    perm = np.zeros((TILE, TILE), np.float32)
    perm[order, np.arange(TILE)] = 1.0
    perms = np.stack([perm, perm.T]).astype(jnp.bfloat16)
    return mats, perms


def split(x):
    high = x.astype(jnp.bfloat16)
    low = (x - high.astype(jnp.float32)).astype(jnp.bfloat16)
    return high, low


def dot(a, b):
    return jnp.dot(a, b, preferred_element_type=jnp.float32)


def mm_right(x, high, low):
    xh, xl = split(x)
    return dot(xh, high) + (dot(xl, high) + dot(xh, low))


def mm_left(high, low, x):
    xh, xl = split(x)
    return dot(high, xh) + (dot(high, xl) + dot(low, xh))


def transform(src, dst, mats, which, pre, post):
    def one(w, carry):
        xr, xi = src[w, 0], src[w, 1]
        r0, r1, i0, i1 = xr[:, :HALF], xr[:, HALF:], xi[:, :HALF], xi[:, HALF:]
        if pre:
            r0, r1, i0, i1 = r0 + r1, r0 - r1, i0 + i1, i0 - i1
        ys = mm_right(jnp.concatenate([r0, i0], 1), mats[which, 0, 0, 0], mats[which, 0, 0, 1])
        yd = mm_right(jnp.concatenate([r1, i1], 1), mats[which, 1, 0, 0], mats[which, 1, 0, 1])
        if post:
            ys, yd = ys + yd, ys - yd
        yr = jnp.concatenate([ys[:, :HALF], yd[:, :HALF]], 1)
        yi = jnp.concatenate([ys[:, HALF:], yd[:, HALF:]], 1)
        r0, r1, i0, i1 = yr[:HALF], yr[HALF:], yi[:HALF], yi[HALF:]
        if pre:
            r0, r1, i0, i1 = r0 + r1, r0 - r1, i0 + i1, i0 - i1
        zs = mm_left(mats[which, 0, 1, 0], mats[which, 0, 1, 1], jnp.concatenate([r0, i0], 0))
        zd = mm_left(mats[which, 1, 1, 0], mats[which, 1, 1, 1], jnp.concatenate([r1, i1], 0))
        if post:
            zs, zd = zs + zd, zs - zd
        dst[w, 0, :HALF, :] = zs[:HALF]
        dst[w, 0, HALF:, :] = zd[:HALF]
        dst[w, 1, :HALF, :] = zs[HALF:]
        dst[w, 1, HALF:, :] = zd[HALF:]
        return carry

    lax.fori_loop(0, 2, one, 0, unroll=True)


ROWS = 32


def rows_loop(count, fn):
    def step(k, carry):
        fn(pl.multiple_of(k * ROWS, ROWS))
        return carry

    lax.fori_loop(0, count // ROWS, step, 0, unroll=8 if count == TILE else 4)


def kernel(
    n_row, n_col,
    pos_any, obj_ref, probe_ref, amp_ref, mats_ref, perms_ref,
    out_ref,
    pad0, pad1, tot0, tot1, gbuf, probe, amp, mats, perms, amp_p, x_ref, b_ref, t_ref,
    r_in, r_x, r_c, r_d, r_f, r_v,
    pos_ref, local_sem, g_send, g_recv, s_send, s_recv,
):
    i, j = lax.axis_index("row"), lax.axis_index("col")
    core = lax.rem(i, 2)
    c = lax.rem(lax.div(i, 2), 2)
    i_in = i + 1 - 2 * core
    i_x = i - 1 + 2 * core
    j_v = j - 1 + 2 * c
    j_f = j + 1 - 2 * c
    has_x = jnp.logical_and(i_x >= 0, i_x < n_row)
    has_v = jnp.logical_and(j_v >= 0, j_v < n_col)
    has_f = jnp.logical_and(j_f >= 0, j_f < n_col)
    has_d = jnp.logical_and(has_x, has_v)
    ix = jnp.clip(i_x, 0, n_row - 1)
    jv = jnp.clip(j_v, 0, n_col - 1)
    jf = jnp.clip(j_f, 0, n_col - 1)
    always = None
    pads, tots = (pad0, pad1), (tot0, tot1)

    def at(start):
        return pl.ds(pl.multiple_of(start, HALF), HALF)

    x_rows, in_rows = at(HALF * core), at(HALF * (1 - core))
    x_rows_p, in_rows_p = at(MARGIN + HALF * core), at(MARGIN + HALF * (1 - core))

    barrier = pltpu.get_barrier_semaphore()

    def when(cond, fn):
        if cond is None:
            fn()
        else:
            pl.when(cond)(fn)

    partners = ((None, (i_in, j)), (has_x, (ix, j)), (has_d, (ix, jv)), (has_v, (i, jv)), (has_f, (i, jf)))
    for cond, dev in partners:
        when(cond, lambda dev=dev: pl.semaphore_signal(barrier, inc=1, device_id=dev, device_id_type=MESH))
    one = lambda cond: cond.astype(jnp.int32)
    pl.semaphore_wait(barrier, 1 + one(has_x) + one(has_d) + one(has_v) + one(has_f))

    def gather(s):
        pad = pads[s]
        dst_x, dst_in = at(3 * HALF * (1 - core)), at(3 * HALF * core)
        f_src, f_dst = at(HALF * (1 - c)), 3 * c
        v_src, v_dst = at(HALF * c), 3 * (1 - c)
        west, east = pl.ds(0, HALF), pl.ds(HALF, HALF)
        obj = obj_ref.at[s]
        table = {
            G_FX: (has_f, has_v, obj.at[:, x_rows, f_src], pad.at[:, f_dst, x_rows_p, :], (i, jf)),
            G_FI: (has_f, has_v, obj.at[:, in_rows, f_src], pad.at[:, f_dst, in_rows_p, :], (i, jf)),
            G_VX: (has_v, has_f, obj.at[:, x_rows, v_src], pad.at[:, v_dst, x_rows_p, :], (i, jv)),
            G_VI: (has_v, has_f, obj.at[:, in_rows, v_src], pad.at[:, v_dst, in_rows_p, :], (i, jv)),
            G_CROSS: (has_x, has_x, obj.at[:, x_rows, west], pad.at[:, 1, dst_x, :], (ix, j)),
            G_CROSS2: (has_x, has_x, obj.at[:, x_rows, east], pad.at[:, 2, dst_x, :], (ix, j)),
            G_DIRECT: (has_d, has_d, obj.at[:, x_rows, v_src], pad.at[:, v_dst, dst_x, :], (ix, jv)),
            G_FWD: (has_x, has_x, pad.at[:, f_dst, x_rows_p, :], pad.at[:, f_dst, dst_x, :], (ix, j)),
            G_IN: (always, always, obj.at[:, in_rows, west], pad.at[:, 1, dst_in, :], (i_in, j)),
            G_IN2: (always, always, obj.at[:, in_rows, east], pad.at[:, 2, dst_in, :], (i_in, j)),
            G_INF: (always, always, pad.at[:, f_dst, in_rows_p, :], pad.at[:, f_dst, dst_in, :], (i_in, j)),
            G_INV: (always, always, pad.at[:, v_dst, in_rows_p, :], pad.at[:, v_dst, dst_in, :], (i_in, j)),
        }
        return {
            k: (sent, comes, pltpu.make_async_remote_copy(
                src_ref=src, dst_ref=dst, send_sem=g_send.at[s, k], recv_sem=g_recv.at[s, k],
                device_id=dev, device_id_type=MESH))
            for k, (sent, comes, src, dst, dev) in table.items()
        }

    def start(copies, *keys):
        for k in keys:
            sent, _, copy = copies[k]
            when(sent, copy.start)

    def arrived(copies, *keys):
        for k in keys:
            _, comes, copy = copies[k]
            when(comes, copy.wait_recv)

    def left(copies, *keys):
        for k in keys:
            sent, _, copy = copies[k]
            when(sent, copy.wait_send)

    g0, g1 = gather(0), gather(1)
    inner_first = (G_FI, G_VI, G_IN, G_IN2)
    then = (G_CROSS, G_CROSS2, G_VX, G_DIRECT)
    start(g0, G_FX)
    start(g1, G_FX)
    start(g0, *inner_first, *then)

    inner = pl.ds(MARGIN, TILE)
    locals_ = [
        pltpu.make_async_copy(obj_ref.at[s, :, :, pl.ds(HALF * k, HALF)], pad.at[:, 1 + k, inner, :], local_sem.at[4 + 2 * s + k])
        for s, pad in enumerate(pads)
        for k in range(2)
    ] + [
        pltpu.make_async_copy(pos_any, pos_ref, local_sem.at[8]),
        pltpu.make_async_copy(probe_ref, probe, local_sem.at[0]),
        pltpu.make_async_copy(amp_ref, amp, local_sem.at[1]),
        pltpu.make_async_copy(mats_ref, mats, local_sem.at[2]),
        pltpu.make_async_copy(perms_ref, perms, local_sem.at[3]),
    ]
    for copy in locals_:
        copy.start()

    start(g1, *inner_first)

    def zero(cond, row0, count, blocks):
        def chunk(r):
            for pad in pads:
                for k in blocks:
                    pad[:, k, pl.ds(pl.multiple_of(row0 + r, ROWS), ROWS), :] = jnp.zeros((2, ROWS, HALF), jnp.float32)

        @pl.when(jnp.logical_not(cond))
        def _():
            rows_loop(count, chunk)

    zero(has_v, MARGIN, TILE, (3 * c,))
    zero(has_f, MARGIN, TILE, (3 * (1 - c),))
    zero(has_d, 3 * HALF * core, HALF, (3 * c,))
    zero(has_x, 3 * HALF * core, HALF, (1, 2, 3 * (1 - c)))

    def clear(r):
        for w in range(2):
            gbuf[w, :, :, pl.ds(r, ROWS), :] = jnp.zeros((2, 5, ROWS, HALF), jnp.float32)

    rows_loop(3 * TILE, clear)
    for copy in locals_[6:]:
        copy.wait()

    def order(w, carry):
        rest = amp[w]
        total = None
        for _ in range(3):
            piece = rest.astype(jnp.bfloat16)
            rest = rest - piece.astype(jnp.float32)
            part = dot(perms[1], dot(piece, perms[0]).astype(jnp.bfloat16))
            total = part if total is None else total + part
        amp_p[w] = total
        return carry

    lax.fori_loop(0, 2, order, 0)
    for copy in locals_[:6]:
        copy.wait()

    lane = lax.broadcasted_iota(jnp.int32, (ROWS, HALF), 1)

    def place(w):
        y, x = pos_ref[0, 0, w, 0, 0], pos_ref[0, 0, w, 0, 1]
        q = jnp.minimum(lax.div(x, HALF), 1)
        return y, q, x - q * HALF

    def window(pad, w, part, r):
        y, block, s = place(w)
        turn = lax.rem(HALF - s, HALF)
        v = [pltpu.roll(pad[part, block + k, pl.ds(y + r, ROWS), :], turn, 1) for k in range(3)]
        own = lane < HALF - s
        return jnp.concatenate([jnp.where(own, v[0], v[1]), jnp.where(own, v[1], v[2])], 1)

    def finish_gather(copies):
        arrived(copies, G_FI)
        start(copies, G_INF)
        arrived(copies, G_VI)
        start(copies, G_INV)
        arrived(copies, G_VX, G_CROSS, G_CROSS2, G_DIRECT, G_IN, G_IN2, G_FWD, G_INF, G_INV)

    for copies in (g0, g1):
        arrived(copies, G_FX)
        start(copies, G_FWD)
    finish_gather(g0)
    start(g1, *then)

    for w in range(2):
        def enter(r, w=w):
            rows = pl.ds(r, ROWS)
            tr, ti = 1.0 + window(pad0, w, 0, r), window(pad0, w, 1, r)
            pr, pi = probe[0, rows, :], probe[1, rows, :]
            x_ref[w, 0, rows, :] = pr * tr - pi * ti
            x_ref[w, 1, rows, :] = pr * ti + pi * tr

        rows_loop(TILE, enter)
    transform(x_ref, b_ref, mats, T_A, True, True)

    finish_gather(g1)

    for w in range(2):
        def leave(r, w=w):
            rows = pl.ds(r, ROWS)
            tr, ti = 1.0 + window(pad1, w, 0, r), window(pad1, w, 1, r)
            t_ref[w, 0, rows, :] = tr
            t_ref[w, 1, rows, :] = ti
            br, bi = b_ref[w, 0, rows, :], b_ref[w, 1, rows, :]
            x_ref[w, 0, rows, :] = br * tr - bi * ti
            x_ref[w, 1, rows, :] = br * ti + bi * tr

        rows_loop(TILE, leave)
    transform(x_ref, x_ref, mats, T_F, True, False)

    for w in range(2):
        def residual(r, w=w):
            rows = pl.ds(r, ROWS)
            fr, fi = x_ref[w, 0, rows, :], x_ref[w, 1, rows, :]
            keep = 1.0 - amp_p[w, rows, :] * lax.rsqrt(fr * fr + fi * fi + 1.0)
            x_ref[w, 0, rows, :] = fr * keep
            x_ref[w, 1, rows, :] = fi * keep

        rows_loop(TILE, residual)
    transform(x_ref, x_ref, mats, T_FI, False, True)

    def turned(w, part, r, v):
        _, _, s = place(w)
        turn = lax.rem(s, HALF)
        a, b = (pltpu.roll(v[:, HALF * k : HALF * (k + 1)], turn, 1) for k in range(2))
        own = lane >= s
        rows = pl.ds(TILE + r, ROWS)
        gbuf[w, part, 1, rows, :] = jnp.where(own, a, 0.0)
        gbuf[w, part, 2, rows, :] = jnp.where(own, b, a)
        gbuf[w, part, 3, rows, :] = jnp.where(own, 0.0, b)

    def add_up(tot, row0, count, blocks):
        def chunk(r):
            r = pl.multiple_of(row0 + r, ROWS)
            for part in range(2):
                for k in blocks:
                    total = None
                    for w in range(2):
                        y, block, _ = place(w)
                        v = gbuf[w, part, 1 - block + k, pl.ds(TILE - y + r, ROWS), :]
                        total = v if total is None else total + v
                    tot[part, k, pl.ds(r, ROWS), :] = total

        rows_loop(count, chunk)

    def scatter(s):
        tot = tots[s]
        cross_rows, inner_rows = at(3 * HALF * core), at(3 * HALF * (1 - core))
        f_blk, v_blk = 3 * (1 - c), 3 * c
        table = {
            S_CORNER: (has_x, has_x, tot.at[:, f_blk, cross_rows, :], r_c.at[s], (ix, j)),
            S_CROSS: (has_x, has_x, tot.at[:, pl.ds(1, 2), cross_rows, :], r_x.at[s], (ix, j)),
            S_DIRECT: (has_d, has_d, tot.at[:, v_blk, cross_rows, :], r_d.at[s], (ix, jv)),
            S_IN: (always, always, tot.at[:, :, inner_rows, :], r_in.at[s], (i_in, j)),
            S_FX: (has_f, has_v, tot.at[:, f_blk, x_rows_p, :], r_f.at[s, :, x_rows, :], (i, jf)),
            S_FI: (has_f, has_v, tot.at[:, f_blk, in_rows_p, :], r_f.at[s, :, in_rows, :], (i, jf)),
            S_VX: (has_v, has_f, tot.at[:, v_blk, x_rows_p, :], r_v.at[s, :, x_rows, :], (i, jv)),
            S_VI: (has_v, has_f, tot.at[:, v_blk, in_rows_p, :], r_v.at[s, :, in_rows, :], (i, jv)),
        }
        return {
            k: (sent, comes, pltpu.make_async_remote_copy(
                src_ref=src, dst_ref=dst, send_sem=s_send.at[s, k], recv_sem=s_recv.at[s, k],
                device_id=dev, device_id_type=MESH))
            for k, (sent, comes, src, dst, dev) in table.items()
        }

    def add_in(s):
        tot = tots[s]

        def chunk(r):
            rows = pl.ds(pl.multiple_of(MARGIN + HALF * (1 - core) + r, ROWS), ROWS)
            tot[:, :, rows, :] = tot[:, :, rows, :] + r_in[s, :, :, pl.ds(r, ROWS), :]

        rows_loop(HALF, chunk)

    def add_corner(s):
        tot = tots[s]

        def chunk(r):
            rows = pl.ds(pl.multiple_of(MARGIN + HALF * core + r, ROWS), ROWS)
            tot[:, 3 * c, rows, :] = tot[:, 3 * c, rows, :] + r_c[s, :, pl.ds(r, ROWS), :]

        @pl.when(has_x)
        def _():
            rows_loop(HALF, chunk)

    def send_early(s, copies):
        everywhere = range(4)
        add_up(tots[s], 3 * HALF * core, HALF, everywhere)
        start(copies, S_CORNER, S_CROSS, S_DIRECT)
        add_up(tots[s], MARGIN, TILE, (0, 3))
        start(copies, S_FX)
        add_up(tots[s], 3 * HALF * (1 - core), HALF, everywhere)
        start(copies, S_IN)
        add_up(tots[s], MARGIN, TILE, (1, 2))

    def send_inner(s, copies):
        arrived(copies, S_IN)
        add_in(s)
        start(copies, S_FI, S_VI)

    def send_late(s, copies):
        arrived(copies, S_CORNER)
        add_corner(s)
        start(copies, S_VX)

    def own_part(s):
        def chunk(r):
            rows, rows_p = pl.ds(r, ROWS), pl.ds(MARGIN + r, ROWS)
            for k in range(2):
                cols = slice(HALF * k, HALF * (k + 1))
                out_ref[s, :, rows, cols] = pads[s][:, 1 + k, rows_p, :] - STEP * tots[s][:, 1 + k, rows_p, :]

        rows_loop(TILE, chunk)

    def take(s, copies, key, cond, rows0, cols, part):
        if key is not None:
            arrived(copies, key)

        def chunk(r):
            rows = pl.ds(pl.multiple_of(rows0 + r, ROWS), ROWS)
            out_ref[s, :, rows, cols] = out_ref[s, :, rows, cols] - STEP * part(r)

        @pl.when(cond)
        def _():
            rows_loop(HALF, chunk)

    def finish(s, copies):
        x0, in0 = HALF * core, HALF * (1 - core)
        f_cols, v_cols = at(HALF * c), at(HALF * (1 - c))
        west, east = slice(0, HALF), slice(HALF, TILE)
        take(s, copies, S_DIRECT, has_d, x0, f_cols, lambda r: r_d[s, :, pl.ds(r, ROWS), :])
        take(s, copies, S_CROSS, has_x, x0, west, lambda r: r_x[s, :, 0, pl.ds(r, ROWS), :])
        take(s, copies, None, has_x, x0, east, lambda r: r_x[s, :, 1, pl.ds(r, ROWS), :])
        take(s, copies, S_FX, has_v, x0, f_cols, lambda r: r_f[s, :, pl.ds(pl.multiple_of(x0 + r, ROWS), ROWS), :])
        take(s, copies, S_FI, has_v, in0, f_cols, lambda r: r_f[s, :, pl.ds(pl.multiple_of(in0 + r, ROWS), ROWS), :])
        take(s, copies, S_VI, has_f, in0, v_cols, lambda r: r_v[s, :, pl.ds(pl.multiple_of(in0 + r, ROWS), ROWS), :])
        take(s, copies, S_VX, has_f, x0, v_cols, lambda r: r_v[s, :, pl.ds(pl.multiple_of(x0 + r, ROWS), ROWS), :])

    for w in range(2):
        def second(r, w=w):
            rows = pl.ds(r, ROWS)
            br, bi = b_ref[w, 0, rows, :], b_ref[w, 1, rows, :]
            cr, ci = x_ref[w, 0, rows, :], x_ref[w, 1, rows, :]
            turned(w, 0, r, br * cr + bi * ci)
            turned(w, 1, r, br * ci - bi * cr)

        rows_loop(TILE, second)
    s1 = scatter(1)
    send_early(1, s1)

    for w in range(2):
        def back(r, w=w):
            rows = pl.ds(r, ROWS)
            tr, ti = t_ref[w, 0, rows, :], t_ref[w, 1, rows, :]
            cr, ci = x_ref[w, 0, rows, :], x_ref[w, 1, rows, :]
            x_ref[w, 0, rows, :] = tr * cr + ti * ci
            x_ref[w, 1, rows, :] = tr * ci - ti * cr

        rows_loop(TILE, back)
    send_inner(1, s1)
    send_late(1, s1)
    transform(x_ref, x_ref, mats, T_AC, True, True)
    for w in range(2):
        def first_slice(r, w=w):
            rows = pl.ds(r, ROWS)
            pr, pi = probe[0, rows, :], probe[1, rows, :]
            cr, ci = x_ref[w, 0, rows, :], x_ref[w, 1, rows, :]
            turned(w, 0, r, pr * cr + pi * ci)
            turned(w, 1, r, pr * ci - pi * cr)

        rows_loop(TILE, first_slice)
    s0 = scatter(0)
    send_early(0, s0)
    send_inner(0, s0)
    send_late(0, s0)
    own_part(1)
    own_part(0)
    finish(1, s1)
    finish(0, s0)
    for copies in (g0, g1, s0, s1):
        left(copies, *copies)


def body(n_row, n_col, mats, perms, obj, probe, amplitude, positions):
    any_space = pl.BlockSpec(memory_space=pltpu.HBM)
    vmem = pl.BlockSpec(memory_space=pltpu.VMEM)
    f32 = jnp.float32
    wide = pltpu.VMEM((2, 4, WIDE, HALF), f32)
    field = pltpu.VMEM((2, 2, TILE, TILE), f32)
    return pl.pallas_call(
        functools.partial(kernel, n_row, n_col),
        out_shape=pltpu.VMEM((2, 2, TILE, TILE), f32),
        in_specs=[any_space] * 6,
        out_specs=vmem,
        scratch_shapes=[
            wide, wide, wide, wide,
            pltpu.VMEM((2, 2, 5, 3 * TILE, HALF), f32),
            pltpu.VMEM((2, TILE, TILE), f32),
            pltpu.VMEM((2, TILE, TILE), f32),
            pltpu.VMEM(mats.shape, jnp.bfloat16),
            pltpu.VMEM(perms.shape, jnp.bfloat16),
            pltpu.VMEM((2, TILE, TILE), f32),
            field, field, field,
            pltpu.VMEM((2, 2, 4, HALF, HALF), f32),
            pltpu.VMEM((2, 2, 2, HALF, HALF), f32),
            pltpu.VMEM((2, 2, HALF, HALF), f32),
            pltpu.VMEM((2, 2, HALF, HALF), f32),
            pltpu.VMEM((2, 2, TILE, HALF), f32),
            pltpu.VMEM((2, 2, TILE, HALF), f32),
            pltpu.SMEM((1, 1, 2, 1, 2), jnp.int32),
            pltpu.SemaphoreType.DMA((9,)),
            pltpu.SemaphoreType.DMA((2, 12)),
            pltpu.SemaphoreType.DMA((2, 12)),
            pltpu.SemaphoreType.DMA((2, 8)),
            pltpu.SemaphoreType.DMA((2, 8)),
        ],
        compiler_params=pltpu.CompilerParams(
            collective_id=0, has_side_effects=True, vmem_limit_bytes=54 * 1024 * 1024
        ),
        cost_estimate=pl.CostEstimate(flops=3 * 10**9, bytes_accessed=8 * 10**6, transcendentals=131072),
    )(positions, obj, probe, amplitude.reshape(2, TILE, TILE), mats, perms)


def solution(mesh):
    mats, perms = constants()
    mats, perms = jnp.asarray(mats), jnp.asarray(perms)
    placed = (
        P(None, None, "row", "col"),
        P(),
        P("row", "col", None, None, None, None),
        P("row", "col", None, None, None),
    )
    return jax.shard_map(
        functools.partial(body, mesh.shape["row"], mesh.shape["col"], mats, perms),
        mesh=mesh, in_specs=placed, out_specs=P(None, None, "row", "col"), check_vma=False,
    )
```

```python
import functools
import math

import jax
import jax.numpy as jnp
import numpy as np
from jax import lax
from jax.experimental import pallas as pl
from jax.experimental.pallas import tpu as pltpu
from jax.sharding import PartitionSpec as P

TILE = 256
MARGIN = 128
HALF = 128
WIDE = 512
STEP = 0.5
MESH = pl.DeviceIdType.MESH

G_FX, G_FI, G_VX, G_VI, G_CROSS, G_CROSS2, G_DIRECT, G_FWD, G_IN, G_IN2, G_INF, G_INV = range(12)
S_CORNER, S_CROSS, S_DIRECT, S_IN, S_FX, S_FI, S_VX, S_VI = range(8)

T_A, T_F, T_FI, T_AC = range(4)


def real_form(m):
    return np.block([[m.real, m.imag], [-m.imag, m.real]])


def matrices():
    n = np.arange(TILE)
    f = np.where(n < TILE // 2, n, n - TILE)
    h = np.exp(-1j * math.pi * ((f * f) % (4 * TILE)) / (2 * TILE))
    dft = np.exp(-2j * math.pi * ((n[:, None] * n[None, :]) % TILE) / TILE) / math.sqrt(TILE)
    spread = np.conj(dft) @ (h[:, None] * dft)
    c0, c1 = spread[:HALF, :HALF], spread[:HALF, HALF:]
    a = [(c0 + c1) / 2, (c0 - c1) / 2]
    fwd = [dft[:HALF, 0::2], dft[:HALF, 1::2]]
    inv = [np.conj(m.T) for m in fwd]
    ac = [np.conj(m) for m in a]
    return np.stack([np.stack([real_form(m) for m in pair]) for pair in (a, fwd, inv, ac)])


def constants():
    right = matrices()
    both = np.stack([right, np.swapaxes(right, -1, -2)], 2)
    both = both.astype(np.float32)
    high = both.astype(jnp.bfloat16)
    low = (both - high.astype(np.float32)).astype(jnp.bfloat16)
    mats = np.stack([high, low], 3)
    order = np.concatenate([np.arange(0, TILE, 2), np.arange(1, TILE, 2)])
    perm = np.zeros((TILE, TILE), np.float32)
    perm[order, np.arange(TILE)] = 1.0
    perms = np.stack([perm, perm.T]).astype(jnp.bfloat16)
    return mats, perms


def split(x):
    high = x.astype(jnp.bfloat16)
    low = (x - high.astype(jnp.float32)).astype(jnp.bfloat16)
    return high, low


def dot(a, b):
    return jnp.dot(a, b, preferred_element_type=jnp.float32)


def mm_right(x, high, low):
    xh, xl = split(x)
    return dot(xh, high) + (dot(xl, high) + dot(xh, low))


def mm_left(high, low, x):
    xh, xl = split(x)
    return dot(high, xh) + (dot(high, xl) + dot(low, xh))


def transform(src, dst, mats, which, pre, post):
    def one(w, carry):
        xr, xi = src[w, 0], src[w, 1]
        r0, r1, i0, i1 = xr[:, :HALF], xr[:, HALF:], xi[:, :HALF], xi[:, HALF:]
        if pre:
            r0, r1, i0, i1 = r0 + r1, r0 - r1, i0 + i1, i0 - i1
        ys = mm_right(jnp.concatenate([r0, i0], 1), mats[which, 0, 0, 0], mats[which, 0, 0, 1])
        yd = mm_right(jnp.concatenate([r1, i1], 1), mats[which, 1, 0, 0], mats[which, 1, 0, 1])
        if post:
            ys, yd = ys + yd, ys - yd
        yr = jnp.concatenate([ys[:, :HALF], yd[:, :HALF]], 1)
        yi = jnp.concatenate([ys[:, HALF:], yd[:, HALF:]], 1)
        r0, r1, i0, i1 = yr[:HALF], yr[HALF:], yi[:HALF], yi[HALF:]
        if pre:
            r0, r1, i0, i1 = r0 + r1, r0 - r1, i0 + i1, i0 - i1
        zs = mm_left(mats[which, 0, 1, 0], mats[which, 0, 1, 1], jnp.concatenate([r0, i0], 0))
        zd = mm_left(mats[which, 1, 1, 0], mats[which, 1, 1, 1], jnp.concatenate([r1, i1], 0))
        if post:
            zs, zd = zs + zd, zs - zd
        dst[w, 0, :HALF, :] = zs[:HALF]
        dst[w, 0, HALF:, :] = zd[:HALF]
        dst[w, 1, :HALF, :] = zs[HALF:]
        dst[w, 1, HALF:, :] = zd[HALF:]
        return carry

    lax.fori_loop(0, 2, one, 0, unroll=True)


ROWS = 32


def rows_loop(count, fn):
    def step(k, carry):
        fn(pl.multiple_of(k * ROWS, ROWS))
        return carry

    lax.fori_loop(0, count // ROWS, step, 0, unroll=8 if count == TILE else 4)


def kernel(
    n_row, n_col,
    pos_any, obj_ref, probe_ref, amp_ref, mats_ref, perms_ref,
    out_ref,
    pad0, pad1, tot0, tot1, gbuf, probe, amp, mats, perms, amp_p, x_ref, b_ref, t_ref,
    r_in, r_x, r_c, r_d, r_f, r_v,
    pos_ref, local_sem, g_send, g_recv, s_send, s_recv,
):
    i, j = lax.axis_index("row"), lax.axis_index("col")
    core = lax.rem(i, 2)
    c = lax.rem(lax.div(i, 2), 2)
    i_in = i + 1 - 2 * core
    i_x = i - 1 + 2 * core
    j_v = j - 1 + 2 * c
    j_f = j + 1 - 2 * c
    has_x = jnp.logical_and(i_x >= 0, i_x < n_row)
    has_v = jnp.logical_and(j_v >= 0, j_v < n_col)
    has_f = jnp.logical_and(j_f >= 0, j_f < n_col)
    has_d = jnp.logical_and(has_x, has_v)
    ix = jnp.clip(i_x, 0, n_row - 1)
    jv = jnp.clip(j_v, 0, n_col - 1)
    jf = jnp.clip(j_f, 0, n_col - 1)
    always = None
    pads, tots = (pad0, pad1), (tot0, tot1)

    def at(start):
        return pl.ds(pl.multiple_of(start, HALF), HALF)

    x_rows, in_rows = at(HALF * core), at(HALF * (1 - core))
    x_rows_p, in_rows_p = at(MARGIN + HALF * core), at(MARGIN + HALF * (1 - core))

    barrier = pltpu.get_barrier_semaphore()

    def when(cond, fn):
        if cond is None:
            fn()
        else:
            pl.when(cond)(fn)

    partners = ((None, (i_in, j)), (has_x, (ix, j)), (has_d, (ix, jv)), (has_v, (i, jv)), (has_f, (i, jf)))
    for cond, dev in partners:
        when(cond, lambda dev=dev: pl.semaphore_signal(barrier, inc=1, device_id=dev, device_id_type=MESH))
    one = lambda cond: cond.astype(jnp.int32)
    pl.semaphore_wait(barrier, 1 + one(has_x) + one(has_d) + one(has_v) + one(has_f))

    def gather(s):
        pad = pads[s]
        dst_x, dst_in = at(3 * HALF * (1 - core)), at(3 * HALF * core)
        f_src, f_dst = at(HALF * (1 - c)), 3 * c
        v_src, v_dst = at(HALF * c), 3 * (1 - c)
        west, east = pl.ds(0, HALF), pl.ds(HALF, HALF)
        obj = obj_ref.at[s]
        table = {
            G_FX: (has_f, has_v, obj.at[:, x_rows, f_src], pad.at[:, f_dst, x_rows_p, :], (i, jf)),
            G_FI: (has_f, has_v, obj.at[:, in_rows, f_src], pad.at[:, f_dst, in_rows_p, :], (i, jf)),
            G_VX: (has_v, has_f, obj.at[:, x_rows, v_src], pad.at[:, v_dst, x_rows_p, :], (i, jv)),
            G_VI: (has_v, has_f, obj.at[:, in_rows, v_src], pad.at[:, v_dst, in_rows_p, :], (i, jv)),
            G_CROSS: (has_x, has_x, obj.at[:, x_rows, west], pad.at[:, 1, dst_x, :], (ix, j)),
            G_CROSS2: (has_x, has_x, obj.at[:, x_rows, east], pad.at[:, 2, dst_x, :], (ix, j)),
            G_DIRECT: (has_d, has_d, obj.at[:, x_rows, v_src], pad.at[:, v_dst, dst_x, :], (ix, jv)),
            G_FWD: (has_x, has_x, pad.at[:, f_dst, x_rows_p, :], pad.at[:, f_dst, dst_x, :], (ix, j)),
            G_IN: (always, always, obj.at[:, in_rows, west], pad.at[:, 1, dst_in, :], (i_in, j)),
            G_IN2: (always, always, obj.at[:, in_rows, east], pad.at[:, 2, dst_in, :], (i_in, j)),
            G_INF: (always, always, pad.at[:, f_dst, in_rows_p, :], pad.at[:, f_dst, dst_in, :], (i_in, j)),
            G_INV: (always, always, pad.at[:, v_dst, in_rows_p, :], pad.at[:, v_dst, dst_in, :], (i_in, j)),
        }
        return {
            k: (sent, comes, pltpu.make_async_remote_copy(
                src_ref=src, dst_ref=dst, send_sem=g_send.at[s, k], recv_sem=g_recv.at[s, k],
                device_id=dev, device_id_type=MESH))
            for k, (sent, comes, src, dst, dev) in table.items()
        }

    def start(copies, *keys):
        for k in keys:
            sent, _, copy = copies[k]
            when(sent, copy.start)

    def arrived(copies, *keys):
        for k in keys:
            _, comes, copy = copies[k]
            when(comes, copy.wait_recv)

    def left(copies, *keys):
        for k in keys:
            sent, _, copy = copies[k]
            when(sent, copy.wait_send)

    g0, g1 = gather(0), gather(1)
    inner_first = (G_FI, G_VI, G_IN, G_IN2)
    then = (G_CROSS, G_CROSS2, G_VX, G_DIRECT)
    start(g0, G_FX)
    start(g1, G_FX)
    start(g0, *inner_first, *then)

    inner = pl.ds(MARGIN, TILE)
    locals_ = [
        pltpu.make_async_copy(obj_ref.at[s, :, :, pl.ds(HALF * k, HALF)], pad.at[:, 1 + k, inner, :], local_sem.at[4 + 2 * s + k])
        for s, pad in enumerate(pads)
        for k in range(2)
    ] + [
        pltpu.make_async_copy(pos_any, pos_ref, local_sem.at[8]),
        pltpu.make_async_copy(probe_ref, probe, local_sem.at[0]),
        pltpu.make_async_copy(amp_ref, amp, local_sem.at[1]),
        pltpu.make_async_copy(mats_ref, mats, local_sem.at[2]),
        pltpu.make_async_copy(perms_ref, perms, local_sem.at[3]),
    ]
    for copy in locals_:
        copy.start()

    start(g1, *inner_first)

    def zero(cond, row0, count, blocks):
        def chunk(r):
            for pad in pads:
                for k in blocks:
                    pad[:, k, pl.ds(pl.multiple_of(row0 + r, ROWS), ROWS), :] = jnp.zeros((2, ROWS, HALF), jnp.float32)

        @pl.when(jnp.logical_not(cond))
        def _():
            rows_loop(count, chunk)

    zero(has_v, MARGIN, TILE, (3 * c,))
    zero(has_f, MARGIN, TILE, (3 * (1 - c),))
    zero(has_d, 3 * HALF * core, HALF, (3 * c,))
    zero(has_x, 3 * HALF * core, HALF, (1, 2, 3 * (1 - c)))

    def clear(r):
        for w in range(2):
            gbuf[w, :, :, pl.ds(r, ROWS), :] = jnp.zeros((2, 5, ROWS, HALF), jnp.float32)

    rows_loop(3 * TILE, clear)
    for copy in locals_[6:]:
        copy.wait()

    def order(w, carry):
        rest = amp[w]
        total = None
        for _ in range(3):
            piece = rest.astype(jnp.bfloat16)
            rest = rest - piece.astype(jnp.float32)
            part = dot(perms[1], dot(piece, perms[0]).astype(jnp.bfloat16))
            total = part if total is None else total + part
        amp_p[w] = total
        return carry

    lax.fori_loop(0, 2, order, 0)
    for copy in locals_[:6]:
        copy.wait()

    lane = lax.broadcasted_iota(jnp.int32, (ROWS, HALF), 1)

    def place(w):
        y, x = pos_ref[0, 0, w, 0, 0], pos_ref[0, 0, w, 0, 1]
        q = jnp.minimum(lax.div(x, HALF), 1)
        return y, q, x - q * HALF

    def window(pad, w, part, r):
        y, block, s = place(w)
        turn = lax.rem(HALF - s, HALF)
        v = [pltpu.roll(pad[part, block + k, pl.ds(y + r, ROWS), :], turn, 1) for k in range(3)]
        own = lane < HALF - s
        return jnp.concatenate([jnp.where(own, v[0], v[1]), jnp.where(own, v[1], v[2])], 1)

    def finish_gather(copies):
        arrived(copies, G_FI)
        start(copies, G_INF)
        arrived(copies, G_VI)
        start(copies, G_INV)
        arrived(copies, G_VX, G_CROSS, G_CROSS2, G_DIRECT, G_IN, G_IN2, G_FWD, G_INF, G_INV)

    for copies in (g0, g1):
        arrived(copies, G_FX)
        start(copies, G_FWD)
    finish_gather(g0)
    start(g1, *then)

    for w in range(2):
        def enter(r, w=w):
            rows = pl.ds(r, ROWS)
            tr, ti = 1.0 + window(pad0, w, 0, r), window(pad0, w, 1, r)
            pr, pi = probe[0, rows, :], probe[1, rows, :]
            x_ref[w, 0, rows, :] = pr * tr - pi * ti
            x_ref[w, 1, rows, :] = pr * ti + pi * tr

        rows_loop(TILE, enter)
    transform(x_ref, b_ref, mats, T_A, True, True)

    finish_gather(g1)

    for w in range(2):
        def leave(r, w=w):
            rows = pl.ds(r, ROWS)
            tr, ti = 1.0 + window(pad1, w, 0, r), window(pad1, w, 1, r)
            t_ref[w, 0, rows, :] = tr
            t_ref[w, 1, rows, :] = ti
            br, bi = b_ref[w, 0, rows, :], b_ref[w, 1, rows, :]
            x_ref[w, 0, rows, :] = br * tr - bi * ti
            x_ref[w, 1, rows, :] = br * ti + bi * tr

        rows_loop(TILE, leave)
    transform(x_ref, x_ref, mats, T_F, True, False)

    for w in range(2):
        def residual(r, w=w):
            rows = pl.ds(r, ROWS)
            fr, fi = x_ref[w, 0, rows, :], x_ref[w, 1, rows, :]
            keep = 1.0 - amp_p[w, rows, :] * lax.rsqrt(fr * fr + fi * fi + 1.0)
            x_ref[w, 0, rows, :] = fr * keep
            x_ref[w, 1, rows, :] = fi * keep

        rows_loop(TILE, residual)
    transform(x_ref, x_ref, mats, T_FI, False, True)

    def turned(w, part, r, v):
        _, _, s = place(w)
        turn = lax.rem(s, HALF)
        a, b = (pltpu.roll(v[:, HALF * k : HALF * (k + 1)], turn, 1) for k in range(2))
        own = lane >= s
        rows = pl.ds(TILE + r, ROWS)
        gbuf[w, part, 1, rows, :] = jnp.where(own, a, 0.0)
        gbuf[w, part, 2, rows, :] = jnp.where(own, b, a)
        gbuf[w, part, 3, rows, :] = jnp.where(own, 0.0, b)

    def add_up(tot, row0, count, blocks):
        def chunk(r):
            r = pl.multiple_of(row0 + r, ROWS)
            for part in range(2):
                for k in blocks:
                    total = None
                    for w in range(2):
                        y, block, _ = place(w)
                        v = gbuf[w, part, 1 - block + k, pl.ds(TILE - y + r, ROWS), :]
                        total = v if total is None else total + v
                    tot[part, k, pl.ds(r, ROWS), :] = total

        rows_loop(count, chunk)

    def scatter(s):
        tot = tots[s]
        cross_rows, inner_rows = at(3 * HALF * core), at(3 * HALF * (1 - core))
        f_blk, v_blk = 3 * (1 - c), 3 * c
        table = {
            S_CORNER: (has_x, has_x, tot.at[:, f_blk, cross_rows, :], r_c.at[s], (ix, j)),
            S_CROSS: (has_x, has_x, tot.at[:, pl.ds(1, 2), cross_rows, :], r_x.at[s], (ix, j)),
            S_DIRECT: (has_d, has_d, tot.at[:, v_blk, cross_rows, :], r_d.at[s], (ix, jv)),
            S_IN: (always, always, tot.at[:, :, inner_rows, :], r_in.at[s], (i_in, j)),
            S_FX: (has_f, has_v, tot.at[:, f_blk, x_rows_p, :], r_f.at[s, :, x_rows, :], (i, jf)),
            S_FI: (has_f, has_v, tot.at[:, f_blk, in_rows_p, :], r_f.at[s, :, in_rows, :], (i, jf)),
            S_VX: (has_v, has_f, tot.at[:, v_blk, x_rows_p, :], r_v.at[s, :, x_rows, :], (i, jv)),
            S_VI: (has_v, has_f, tot.at[:, v_blk, in_rows_p, :], r_v.at[s, :, in_rows, :], (i, jv)),
        }
        return {
            k: (sent, comes, pltpu.make_async_remote_copy(
                src_ref=src, dst_ref=dst, send_sem=s_send.at[s, k], recv_sem=s_recv.at[s, k],
                device_id=dev, device_id_type=MESH))
            for k, (sent, comes, src, dst, dev) in table.items()
        }

    def add_in(s):
        tot = tots[s]

        def chunk(r):
            rows = pl.ds(pl.multiple_of(MARGIN + HALF * (1 - core) + r, ROWS), ROWS)
            tot[:, :, rows, :] = tot[:, :, rows, :] + r_in[s, :, :, pl.ds(r, ROWS), :]

        rows_loop(HALF, chunk)

    def add_corner(s):
        tot = tots[s]

        def chunk(r):
            rows = pl.ds(pl.multiple_of(MARGIN + HALF * core + r, ROWS), ROWS)
            tot[:, 3 * c, rows, :] = tot[:, 3 * c, rows, :] + r_c[s, :, pl.ds(r, ROWS), :]

        @pl.when(has_x)
        def _():
            rows_loop(HALF, chunk)

    def send_early(s, copies):
        everywhere = range(4)
        add_up(tots[s], 3 * HALF * core, HALF, everywhere)
        start(copies, S_CORNER, S_DIRECT)
        if s == 1:
            start(copies, S_CROSS)
        add_up(tots[s], MARGIN, TILE, (0, 3))
        start(copies, S_FX)
        add_up(tots[s], 3 * HALF * (1 - core), HALF, everywhere)
        start(copies, S_IN)
        add_up(tots[s], MARGIN, TILE, (1, 2))

    def send_inner(s, copies):
        arrived(copies, S_IN)
        add_in(s)
        start(copies, S_FI, S_VI)

    def send_late(s, copies):
        arrived(copies, S_CORNER)
        add_corner(s)
        start(copies, S_VX)

    def own_part(s):
        def chunk(r):
            rows, rows_p = pl.ds(r, ROWS), pl.ds(MARGIN + r, ROWS)
            for k in range(2):
                cols = slice(HALF * k, HALF * (k + 1))
                out_ref[s, :, rows, cols] = pads[s][:, 1 + k, rows_p, :] - STEP * tots[s][:, 1 + k, rows_p, :]

        rows_loop(TILE, chunk)

    def take(s, copies, key, cond, rows0, cols, part):
        if key is not None:
            arrived(copies, key)

        def chunk(r):
            rows = pl.ds(pl.multiple_of(rows0 + r, ROWS), ROWS)
            out_ref[s, :, rows, cols] = out_ref[s, :, rows, cols] - STEP * part(r)

        @pl.when(cond)
        def _():
            rows_loop(HALF, chunk)

    def finish(s, copies):
        x0, in0 = HALF * core, HALF * (1 - core)
        f_cols, v_cols = at(HALF * c), at(HALF * (1 - c))
        west, east = slice(0, HALF), slice(HALF, TILE)
        take(s, copies, S_DIRECT, has_d, x0, f_cols, lambda r: r_d[s, :, pl.ds(r, ROWS), :])
        take(s, copies, S_CROSS, has_x, x0, west, lambda r: r_x[s, :, 0, pl.ds(r, ROWS), :])
        take(s, copies, None, has_x, x0, east, lambda r: r_x[s, :, 1, pl.ds(r, ROWS), :])
        take(s, copies, S_FX, has_v, x0, f_cols, lambda r: r_f[s, :, pl.ds(pl.multiple_of(x0 + r, ROWS), ROWS), :])
        take(s, copies, S_FI, has_v, in0, f_cols, lambda r: r_f[s, :, pl.ds(pl.multiple_of(in0 + r, ROWS), ROWS), :])
        take(s, copies, S_VI, has_f, in0, v_cols, lambda r: r_v[s, :, pl.ds(pl.multiple_of(in0 + r, ROWS), ROWS), :])
        take(s, copies, S_VX, has_f, x0, v_cols, lambda r: r_v[s, :, pl.ds(pl.multiple_of(x0 + r, ROWS), ROWS), :])

    for w in range(2):
        def second(r, w=w):
            rows = pl.ds(r, ROWS)
            br, bi = b_ref[w, 0, rows, :], b_ref[w, 1, rows, :]
            cr, ci = x_ref[w, 0, rows, :], x_ref[w, 1, rows, :]
            turned(w, 0, r, br * cr + bi * ci)
            turned(w, 1, r, br * ci - bi * cr)

        rows_loop(TILE, second)
    s1 = scatter(1)
    send_early(1, s1)

    for w in range(2):
        def back(r, w=w):
            rows = pl.ds(r, ROWS)
            tr, ti = t_ref[w, 0, rows, :], t_ref[w, 1, rows, :]
            cr, ci = x_ref[w, 0, rows, :], x_ref[w, 1, rows, :]
            x_ref[w, 0, rows, :] = tr * cr + ti * ci
            x_ref[w, 1, rows, :] = tr * ci - ti * cr

        rows_loop(TILE, back)
    send_inner(1, s1)
    send_late(1, s1)
    transform(x_ref, x_ref, mats, T_AC, True, True)
    for w in range(2):
        def first_slice(r, w=w):
            rows = pl.ds(r, ROWS)
            pr, pi = probe[0, rows, :], probe[1, rows, :]
            cr, ci = x_ref[w, 0, rows, :], x_ref[w, 1, rows, :]
            turned(w, 0, r, pr * cr + pi * ci)
            turned(w, 1, r, pr * ci - pi * cr)

        rows_loop(TILE, first_slice)
    s0 = scatter(0)
    send_early(0, s0)
    send_inner(0, s0)
    left(s1, S_CROSS)
    start(s0, S_CROSS)
    send_late(0, s0)
    own_part(1)
    own_part(0)
    finish(1, s1)
    finish(0, s0)
    for copies in (g0, g1, s0):
        left(copies, *copies)
    left(s1, *(k for k in s1 if k not in (S_CROSS,)))


def body(n_row, n_col, mats, perms, obj, probe, amplitude, positions):
    any_space = pl.BlockSpec(memory_space=pltpu.HBM)
    vmem = pl.BlockSpec(memory_space=pltpu.VMEM)
    f32 = jnp.float32
    wide = pltpu.VMEM((2, 4, WIDE, HALF), f32)
    field = pltpu.VMEM((2, 2, TILE, TILE), f32)
    return pl.pallas_call(
        functools.partial(kernel, n_row, n_col),
        out_shape=pltpu.VMEM((2, 2, TILE, TILE), f32),
        in_specs=[any_space] * 6,
        out_specs=vmem,
        scratch_shapes=[
            wide, wide, wide, wide,
            pltpu.VMEM((2, 2, 5, 3 * TILE, HALF), f32),
            pltpu.VMEM((2, TILE, TILE), f32),
            pltpu.VMEM((2, TILE, TILE), f32),
            pltpu.VMEM(mats.shape, jnp.bfloat16),
            pltpu.VMEM(perms.shape, jnp.bfloat16),
            pltpu.VMEM((2, TILE, TILE), f32),
            field, field, field,
            pltpu.VMEM((2, 2, 4, HALF, HALF), f32),
            pltpu.VMEM((2, 2, 2, HALF, HALF), f32),
            pltpu.VMEM((2, 2, HALF, HALF), f32),
            pltpu.VMEM((2, 2, HALF, HALF), f32),
            pltpu.VMEM((2, 2, TILE, HALF), f32),
            pltpu.VMEM((2, 2, TILE, HALF), f32),
            pltpu.SMEM((1, 1, 2, 1, 2), jnp.int32),
            pltpu.SemaphoreType.DMA((9,)),
            pltpu.SemaphoreType.DMA((2, 12)),
            pltpu.SemaphoreType.DMA((2, 12)),
            pltpu.SemaphoreType.DMA((2, 8)),
            pltpu.SemaphoreType.DMA((2, 8)),
        ],
        compiler_params=pltpu.CompilerParams(
            collective_id=0, has_side_effects=True, vmem_limit_bytes=54 * 1024 * 1024
        ),
        cost_estimate=pl.CostEstimate(flops=3 * 10**9, bytes_accessed=8 * 10**6, transcendentals=131072),
    )(positions, obj, probe, amplitude.reshape(2, TILE, TILE), mats, perms)


def solution(mesh):
    mats, perms = constants()
    mats, perms = jnp.asarray(mats), jnp.asarray(perms)
    placed = (
        P(None, None, "row", "col"),
        P(),
        P("row", "col", None, None, None, None),
        P("row", "col", None, None, None),
    )
    return jax.shard_map(
        functools.partial(body, mesh.shape["row"], mesh.shape["col"], mats, perms),
        mesh=mesh, in_specs=placed, out_specs=P(None, None, "row", "col"), check_vma=False,
    )
```

```python
import functools
import math

import jax
import jax.numpy as jnp
import numpy as np
from jax import lax
from jax.experimental import pallas as pl
from jax.experimental.pallas import tpu as pltpu
from jax.sharding import PartitionSpec as P

TILE = 256
MARGIN = 128
HALF = 128
WIDE = 512
STEP = 0.5
MESH = pl.DeviceIdType.MESH

G_FX, G_FI, G_VX, G_VI, G_CROSS, G_CROSS2, G_DIRECT, G_FWD, G_IN, G_IN2, G_INF, G_INV = range(12)
S_CORNER, S_CROSS, S_DIRECT, S_IN, S_FX, S_FI, S_VX, S_VI = range(8)

T_A, T_F, T_FI, T_AC = range(4)


def real_form(m):
    return np.block([[m.real, m.imag], [-m.imag, m.real]])


def matrices():
    n = np.arange(TILE)
    f = np.where(n < TILE // 2, n, n - TILE)
    h = np.exp(-1j * math.pi * ((f * f) % (4 * TILE)) / (2 * TILE))
    dft = np.exp(-2j * math.pi * ((n[:, None] * n[None, :]) % TILE) / TILE) / math.sqrt(TILE)
    spread = np.conj(dft) @ (h[:, None] * dft)
    c0, c1 = spread[:HALF, :HALF], spread[:HALF, HALF:]
    a = [(c0 + c1) / 2, (c0 - c1) / 2]
    fwd = [dft[:HALF, 0::2], dft[:HALF, 1::2]]
    inv = [np.conj(m.T) for m in fwd]
    ac = [np.conj(m) for m in a]
    return np.stack([np.stack([real_form(m) for m in pair]) for pair in (a, fwd, inv, ac)])


def constants():
    right = matrices()
    both = np.stack([right, np.swapaxes(right, -1, -2)], 2)
    both = both.astype(np.float32)
    high = both.astype(jnp.bfloat16)
    low = (both - high.astype(np.float32)).astype(jnp.bfloat16)
    mats = np.stack([high, low], 3)
    order = np.concatenate([np.arange(0, TILE, 2), np.arange(1, TILE, 2)])
    perm = np.zeros((TILE, TILE), np.float32)
    perm[order, np.arange(TILE)] = 1.0
    perms = np.stack([perm, perm.T]).astype(jnp.bfloat16)
    return mats, perms


def split(x):
    high = x.astype(jnp.bfloat16)
    low = (x - high.astype(jnp.float32)).astype(jnp.bfloat16)
    return high, low


def dot(a, b):
    return jnp.dot(a, b, preferred_element_type=jnp.float32)


def mm_right(x, high, low):
    xh, xl = split(x)
    return dot(xh, high) + (dot(xl, high) + dot(xh, low))


def mm_left(high, low, x):
    xh, xl = split(x)
    return dot(high, xh) + (dot(high, xl) + dot(low, xh))


def transform(src, dst, mats, which, pre, post):
    sums, diffs = [], []
    for w in range(2):
        xr, xi = src[w, 0], src[w, 1]
        r0, r1, i0, i1 = xr[:, :HALF], xr[:, HALF:], xi[:, :HALF], xi[:, HALF:]
        if pre:
            r0, r1, i0, i1 = r0 + r1, r0 - r1, i0 + i1, i0 - i1
        sums.append(jnp.concatenate([r0, i0], 1))
        diffs.append(jnp.concatenate([r1, i1], 1))
    all_s = mm_right(jnp.concatenate(sums, 0), mats[which, 0, 0, 0], mats[which, 0, 0, 1])
    all_d = mm_right(jnp.concatenate(diffs, 0), mats[which, 1, 0, 0], mats[which, 1, 0, 1])
    for w in range(2):
        ys, yd = all_s[TILE * w : TILE * (w + 1)], all_d[TILE * w : TILE * (w + 1)]
        if post:
            ys, yd = ys + yd, ys - yd
        yr = jnp.concatenate([ys[:, :HALF], yd[:, :HALF]], 1)
        yi = jnp.concatenate([ys[:, HALF:], yd[:, HALF:]], 1)
        r0, r1, i0, i1 = yr[:HALF], yr[HALF:], yi[:HALF], yi[HALF:]
        if pre:
            r0, r1, i0, i1 = r0 + r1, r0 - r1, i0 + i1, i0 - i1
        zs = mm_left(mats[which, 0, 1, 0], mats[which, 0, 1, 1], jnp.concatenate([r0, i0], 0))
        zd = mm_left(mats[which, 1, 1, 0], mats[which, 1, 1, 1], jnp.concatenate([r1, i1], 0))
        if post:
            zs, zd = zs + zd, zs - zd
        dst[w, 0, :HALF, :] = zs[:HALF]
        dst[w, 0, HALF:, :] = zd[:HALF]
        dst[w, 1, :HALF, :] = zs[HALF:]
        dst[w, 1, HALF:, :] = zd[HALF:]


ROWS = 32


def rows_loop(count, fn):
    def step(k, carry):
        fn(pl.multiple_of(k * ROWS, ROWS))
        return carry

    lax.fori_loop(0, count // ROWS, step, 0, unroll=8 if count == TILE else 4)


def kernel(
    n_row, n_col,
    pos_any, obj_ref, probe_ref, amp_ref, mats_ref, perms_ref,
    out_ref,
    pad0, pad1, tot0, tot1, gbuf, probe, amp, mats, perms, amp_p, x_ref, b_ref, t_ref,
    r_in, r_x, r_c, r_d, r_f, r_v,
    pos_ref, local_sem, g_send, g_recv, s_send, s_recv,
):
    i, j = lax.axis_index("row"), lax.axis_index("col")
    core = lax.rem(i, 2)
    c = lax.rem(lax.div(i, 2), 2)
    i_in = i + 1 - 2 * core
    i_x = i - 1 + 2 * core
    j_v = j - 1 + 2 * c
    j_f = j + 1 - 2 * c
    has_x = jnp.logical_and(i_x >= 0, i_x < n_row)
    has_v = jnp.logical_and(j_v >= 0, j_v < n_col)
    has_f = jnp.logical_and(j_f >= 0, j_f < n_col)
    has_d = jnp.logical_and(has_x, has_v)
    ix = jnp.clip(i_x, 0, n_row - 1)
    jv = jnp.clip(j_v, 0, n_col - 1)
    jf = jnp.clip(j_f, 0, n_col - 1)
    always = None
    pads, tots = (pad0, pad1), (tot0, tot1)

    def at(start):
        return pl.ds(pl.multiple_of(start, HALF), HALF)

    x_rows, in_rows = at(HALF * core), at(HALF * (1 - core))
    x_rows_p, in_rows_p = at(MARGIN + HALF * core), at(MARGIN + HALF * (1 - core))

    barrier = pltpu.get_barrier_semaphore()

    def when(cond, fn):
        if cond is None:
            fn()
        else:
            pl.when(cond)(fn)

    partners = ((None, (i_in, j)), (has_x, (ix, j)), (has_d, (ix, jv)), (has_v, (i, jv)), (has_f, (i, jf)))
    for cond, dev in partners:
        when(cond, lambda dev=dev: pl.semaphore_signal(barrier, inc=1, device_id=dev, device_id_type=MESH))
    one = lambda cond: cond.astype(jnp.int32)
    pl.semaphore_wait(barrier, 1 + one(has_x) + one(has_d) + one(has_v) + one(has_f))

    def gather(s):
        pad = pads[s]
        dst_x, dst_in = at(3 * HALF * (1 - core)), at(3 * HALF * core)
        f_src, f_dst = at(HALF * (1 - c)), 3 * c
        v_src, v_dst = at(HALF * c), 3 * (1 - c)
        west, east = pl.ds(0, HALF), pl.ds(HALF, HALF)
        obj = obj_ref.at[s]
        table = {
            G_FX: (has_f, has_v, obj.at[:, x_rows, f_src], pad.at[:, f_dst, x_rows_p, :], (i, jf)),
            G_FI: (has_f, has_v, obj.at[:, in_rows, f_src], pad.at[:, f_dst, in_rows_p, :], (i, jf)),
            G_VX: (has_v, has_f, obj.at[:, x_rows, v_src], pad.at[:, v_dst, x_rows_p, :], (i, jv)),
            G_VI: (has_v, has_f, obj.at[:, in_rows, v_src], pad.at[:, v_dst, in_rows_p, :], (i, jv)),
            G_CROSS: (has_x, has_x, obj.at[:, x_rows, west], pad.at[:, 1, dst_x, :], (ix, j)),
            G_CROSS2: (has_x, has_x, obj.at[:, x_rows, east], pad.at[:, 2, dst_x, :], (ix, j)),
            G_DIRECT: (has_d, has_d, obj.at[:, x_rows, v_src], pad.at[:, v_dst, dst_x, :], (ix, jv)),
            G_FWD: (has_x, has_x, pad.at[:, f_dst, x_rows_p, :], pad.at[:, f_dst, dst_x, :], (ix, j)),
            G_IN: (always, always, obj.at[:, in_rows, west], pad.at[:, 1, dst_in, :], (i_in, j)),
            G_IN2: (always, always, obj.at[:, in_rows, east], pad.at[:, 2, dst_in, :], (i_in, j)),
            G_INF: (always, always, pad.at[:, f_dst, in_rows_p, :], pad.at[:, f_dst, dst_in, :], (i_in, j)),
            G_INV: (always, always, pad.at[:, v_dst, in_rows_p, :], pad.at[:, v_dst, dst_in, :], (i_in, j)),
        }
        return {
            k: (sent, comes, pltpu.make_async_remote_copy(
                src_ref=src, dst_ref=dst, send_sem=g_send.at[s, k], recv_sem=g_recv.at[s, k],
                device_id=dev, device_id_type=MESH))
            for k, (sent, comes, src, dst, dev) in table.items()
        }

    def start(copies, *keys):
        for k in keys:
            sent, _, copy = copies[k]
            when(sent, copy.start)

    def arrived(copies, *keys):
        for k in keys:
            _, comes, copy = copies[k]
            when(comes, copy.wait_recv)

    def left(copies, *keys):
        for k in keys:
            sent, _, copy = copies[k]
            when(sent, copy.wait_send)

    g0, g1 = gather(0), gather(1)
    inner_first = (G_FI, G_VI, G_IN, G_IN2)
    then = (G_CROSS, G_CROSS2, G_VX, G_DIRECT)
    start(g0, G_FX)
    start(g1, G_FX)
    start(g0, *inner_first, *then)

    inner = pl.ds(MARGIN, TILE)
    locals_ = [
        pltpu.make_async_copy(obj_ref.at[s, :, :, pl.ds(HALF * k, HALF)], pad.at[:, 1 + k, inner, :], local_sem.at[4 + 2 * s + k])
        for s, pad in enumerate(pads)
        for k in range(2)
    ] + [
        pltpu.make_async_copy(pos_any, pos_ref, local_sem.at[8]),
        pltpu.make_async_copy(probe_ref, probe, local_sem.at[0]),
        pltpu.make_async_copy(amp_ref, amp, local_sem.at[1]),
        pltpu.make_async_copy(mats_ref, mats, local_sem.at[2]),
        pltpu.make_async_copy(perms_ref, perms, local_sem.at[3]),
    ]
    for copy in locals_:
        copy.start()

    start(g1, *inner_first)

    def zero(cond, row0, count, blocks):
        def chunk(r):
            for pad in pads:
                for k in blocks:
                    pad[:, k, pl.ds(pl.multiple_of(row0 + r, ROWS), ROWS), :] = jnp.zeros((2, ROWS, HALF), jnp.float32)

        @pl.when(jnp.logical_not(cond))
        def _():
            rows_loop(count, chunk)

    zero(has_v, MARGIN, TILE, (3 * c,))
    zero(has_f, MARGIN, TILE, (3 * (1 - c),))
    zero(has_d, 3 * HALF * core, HALF, (3 * c,))
    zero(has_x, 3 * HALF * core, HALF, (1, 2, 3 * (1 - c)))

    def clear(r):
        for w in range(2):
            gbuf[w, :, :, pl.ds(r, ROWS), :] = jnp.zeros((2, 5, ROWS, HALF), jnp.float32)

    rows_loop(3 * TILE, clear)
    for copy in locals_[6:]:
        copy.wait()

    def order(w, carry):
        rest = amp[w]
        total = None
        for _ in range(3):
            piece = rest.astype(jnp.bfloat16)
            rest = rest - piece.astype(jnp.float32)
            part = dot(perms[1], dot(piece, perms[0]).astype(jnp.bfloat16))
            total = part if total is None else total + part
        amp_p[w] = total
        return carry

    lax.fori_loop(0, 2, order, 0)
    for copy in locals_[:6]:
        copy.wait()

    lane = lax.broadcasted_iota(jnp.int32, (ROWS, HALF), 1)

    def place(w):
        y, x = pos_ref[0, 0, w, 0, 0], pos_ref[0, 0, w, 0, 1]
        q = jnp.minimum(lax.div(x, HALF), 1)
        return y, q, x - q * HALF

    def window(pad, w, part, r):
        y, block, s = place(w)
        turn = lax.rem(HALF - s, HALF)
        v = [pltpu.roll(pad[part, block + k, pl.ds(y + r, ROWS), :], turn, 1) for k in range(3)]
        own = lane < HALF - s
        return jnp.concatenate([jnp.where(own, v[0], v[1]), jnp.where(own, v[1], v[2])], 1)

    def finish_gather(copies):
        arrived(copies, G_FI)
        start(copies, G_INF)
        arrived(copies, G_VI)
        start(copies, G_INV)
        arrived(copies, G_VX, G_CROSS, G_CROSS2, G_DIRECT, G_IN, G_IN2, G_FWD, G_INF, G_INV)

    for copies in (g0, g1):
        arrived(copies, G_FX)
        start(copies, G_FWD)
    finish_gather(g0)
    start(g1, *then)

    for w in range(2):
        def enter(r, w=w):
            rows = pl.ds(r, ROWS)
            tr, ti = 1.0 + window(pad0, w, 0, r), window(pad0, w, 1, r)
            pr, pi = probe[0, rows, :], probe[1, rows, :]
            x_ref[w, 0, rows, :] = pr * tr - pi * ti
            x_ref[w, 1, rows, :] = pr * ti + pi * tr

        rows_loop(TILE, enter)
    transform(x_ref, b_ref, mats, T_A, True, True)

    finish_gather(g1)

    for w in range(2):
        def leave(r, w=w):
            rows = pl.ds(r, ROWS)
            tr, ti = 1.0 + window(pad1, w, 0, r), window(pad1, w, 1, r)
            t_ref[w, 0, rows, :] = tr
            t_ref[w, 1, rows, :] = ti
            br, bi = b_ref[w, 0, rows, :], b_ref[w, 1, rows, :]
            x_ref[w, 0, rows, :] = br * tr - bi * ti
            x_ref[w, 1, rows, :] = br * ti + bi * tr

        rows_loop(TILE, leave)
    transform(x_ref, x_ref, mats, T_F, True, False)

    for w in range(2):
        def residual(r, w=w):
            rows = pl.ds(r, ROWS)
            fr, fi = x_ref[w, 0, rows, :], x_ref[w, 1, rows, :]
            keep = 1.0 - amp_p[w, rows, :] * lax.rsqrt(fr * fr + fi * fi + 1.0)
            x_ref[w, 0, rows, :] = fr * keep
            x_ref[w, 1, rows, :] = fi * keep

        rows_loop(TILE, residual)
    transform(x_ref, x_ref, mats, T_FI, False, True)

    def turned(w, part, r, v):
        _, _, s = place(w)
        turn = lax.rem(s, HALF)
        a, b = (pltpu.roll(v[:, HALF * k : HALF * (k + 1)], turn, 1) for k in range(2))
        own = lane >= s
        rows = pl.ds(TILE + r, ROWS)
        gbuf[w, part, 1, rows, :] = jnp.where(own, a, 0.0)
        gbuf[w, part, 2, rows, :] = jnp.where(own, b, a)
        gbuf[w, part, 3, rows, :] = jnp.where(own, 0.0, b)

    def add_up(tot, row0, count, blocks):
        def chunk(r):
            r = pl.multiple_of(row0 + r, ROWS)
            for part in range(2):
                for k in blocks:
                    total = None
                    for w in range(2):
                        y, block, _ = place(w)
                        v = gbuf[w, part, 1 - block + k, pl.ds(TILE - y + r, ROWS), :]
                        total = v if total is None else total + v
                    tot[part, k, pl.ds(r, ROWS), :] = total

        rows_loop(count, chunk)

    def scatter(s):
        tot = tots[s]
        cross_rows, inner_rows = at(3 * HALF * core), at(3 * HALF * (1 - core))
        f_blk, v_blk = 3 * (1 - c), 3 * c
        table = {
            S_CORNER: (has_x, has_x, tot.at[:, f_blk, cross_rows, :], r_c.at[s], (ix, j)),
            S_CROSS: (has_x, has_x, tot.at[:, pl.ds(1, 2), cross_rows, :], r_x.at[s], (ix, j)),
            S_DIRECT: (has_d, has_d, tot.at[:, v_blk, cross_rows, :], r_d.at[s], (ix, jv)),
            S_IN: (always, always, tot.at[:, :, inner_rows, :], r_in.at[s], (i_in, j)),
            S_FX: (has_f, has_v, tot.at[:, f_blk, x_rows_p, :], r_f.at[s, :, x_rows, :], (i, jf)),
            S_FI: (has_f, has_v, tot.at[:, f_blk, in_rows_p, :], r_f.at[s, :, in_rows, :], (i, jf)),
            S_VX: (has_v, has_f, tot.at[:, v_blk, x_rows_p, :], r_v.at[s, :, x_rows, :], (i, jv)),
            S_VI: (has_v, has_f, tot.at[:, v_blk, in_rows_p, :], r_v.at[s, :, in_rows, :], (i, jv)),
        }
        return {
            k: (sent, comes, pltpu.make_async_remote_copy(
                src_ref=src, dst_ref=dst, send_sem=s_send.at[s, k], recv_sem=s_recv.at[s, k],
                device_id=dev, device_id_type=MESH))
            for k, (sent, comes, src, dst, dev) in table.items()
        }

    def add_in(s):
        tot = tots[s]

        def chunk(r):
            rows = pl.ds(pl.multiple_of(MARGIN + HALF * (1 - core) + r, ROWS), ROWS)
            tot[:, :, rows, :] = tot[:, :, rows, :] + r_in[s, :, :, pl.ds(r, ROWS), :]

        rows_loop(HALF, chunk)

    def add_corner(s):
        tot = tots[s]

        def chunk(r):
            rows = pl.ds(pl.multiple_of(MARGIN + HALF * core + r, ROWS), ROWS)
            tot[:, 3 * c, rows, :] = tot[:, 3 * c, rows, :] + r_c[s, :, pl.ds(r, ROWS), :]

        @pl.when(has_x)
        def _():
            rows_loop(HALF, chunk)

    def send_early(s, copies):
        everywhere = range(4)
        add_up(tots[s], 3 * HALF * core, HALF, everywhere)
        start(copies, S_CORNER, S_DIRECT)
        if s == 1:
            start(copies, S_CROSS)
        add_up(tots[s], MARGIN, TILE, (0, 3))
        start(copies, S_FX)
        add_up(tots[s], 3 * HALF * (1 - core), HALF, everywhere)
        start(copies, S_IN)
        add_up(tots[s], MARGIN, TILE, (1, 2))

    def send_inner(s, copies):
        arrived(copies, S_IN)
        add_in(s)
        start(copies, S_FI, S_VI)

    def send_late(s, copies):
        arrived(copies, S_CORNER)
        add_corner(s)
        start(copies, S_VX)

    def own_part(s):
        def chunk(r):
            rows, rows_p = pl.ds(r, ROWS), pl.ds(MARGIN + r, ROWS)
            for k in range(2):
                cols = slice(HALF * k, HALF * (k + 1))
                out_ref[s, :, rows, cols] = pads[s][:, 1 + k, rows_p, :] - STEP * tots[s][:, 1 + k, rows_p, :]

        rows_loop(TILE, chunk)

    def take(s, copies, key, cond, rows0, cols, part):
        if key is not None:
            arrived(copies, key)

        def chunk(r):
            rows = pl.ds(pl.multiple_of(rows0 + r, ROWS), ROWS)
            out_ref[s, :, rows, cols] = out_ref[s, :, rows, cols] - STEP * part(r)

        @pl.when(cond)
        def _():
            rows_loop(HALF, chunk)

    def finish(s, copies):
        x0, in0 = HALF * core, HALF * (1 - core)
        f_cols, v_cols = at(HALF * c), at(HALF * (1 - c))
        west, east = slice(0, HALF), slice(HALF, TILE)
        take(s, copies, S_DIRECT, has_d, x0, f_cols, lambda r: r_d[s, :, pl.ds(r, ROWS), :])
        take(s, copies, S_CROSS, has_x, x0, west, lambda r: r_x[s, :, 0, pl.ds(r, ROWS), :])
        take(s, copies, None, has_x, x0, east, lambda r: r_x[s, :, 1, pl.ds(r, ROWS), :])
        take(s, copies, S_FX, has_v, x0, f_cols, lambda r: r_f[s, :, pl.ds(pl.multiple_of(x0 + r, ROWS), ROWS), :])
        take(s, copies, S_FI, has_v, in0, f_cols, lambda r: r_f[s, :, pl.ds(pl.multiple_of(in0 + r, ROWS), ROWS), :])
        take(s, copies, S_VI, has_f, in0, v_cols, lambda r: r_v[s, :, pl.ds(pl.multiple_of(in0 + r, ROWS), ROWS), :])
        take(s, copies, S_VX, has_f, x0, v_cols, lambda r: r_v[s, :, pl.ds(pl.multiple_of(x0 + r, ROWS), ROWS), :])

    for w in range(2):
        def second(r, w=w):
            rows = pl.ds(r, ROWS)
            br, bi = b_ref[w, 0, rows, :], b_ref[w, 1, rows, :]
            cr, ci = x_ref[w, 0, rows, :], x_ref[w, 1, rows, :]
            turned(w, 0, r, br * cr + bi * ci)
            turned(w, 1, r, br * ci - bi * cr)

        rows_loop(TILE, second)
    s1 = scatter(1)
    send_early(1, s1)

    for w in range(2):
        def back(r, w=w):
            rows = pl.ds(r, ROWS)
            tr, ti = t_ref[w, 0, rows, :], t_ref[w, 1, rows, :]
            cr, ci = x_ref[w, 0, rows, :], x_ref[w, 1, rows, :]
            x_ref[w, 0, rows, :] = tr * cr + ti * ci
            x_ref[w, 1, rows, :] = tr * ci - ti * cr

        rows_loop(TILE, back)
    send_inner(1, s1)
    send_late(1, s1)
    transform(x_ref, x_ref, mats, T_AC, True, True)
    for w in range(2):
        def first_slice(r, w=w):
            rows = pl.ds(r, ROWS)
            pr, pi = probe[0, rows, :], probe[1, rows, :]
            cr, ci = x_ref[w, 0, rows, :], x_ref[w, 1, rows, :]
            turned(w, 0, r, pr * cr + pi * ci)
            turned(w, 1, r, pr * ci - pi * cr)

        rows_loop(TILE, first_slice)
    s0 = scatter(0)
    send_early(0, s0)
    send_inner(0, s0)
    left(s1, S_CROSS)
    start(s0, S_CROSS)
    send_late(0, s0)
    own_part(1)
    own_part(0)
    finish(1, s1)
    finish(0, s0)
    for copies in (g0, g1, s0):
        left(copies, *copies)
    left(s1, *(k for k in s1 if k not in (S_CROSS,)))


def body(n_row, n_col, mats, perms, obj, probe, amplitude, positions):
    any_space = pl.BlockSpec(memory_space=pltpu.HBM)
    vmem = pl.BlockSpec(memory_space=pltpu.VMEM)
    f32 = jnp.float32
    wide = pltpu.VMEM((2, 4, WIDE, HALF), f32)
    field = pltpu.VMEM((2, 2, TILE, TILE), f32)
    return pl.pallas_call(
        functools.partial(kernel, n_row, n_col),
        out_shape=pltpu.VMEM((2, 2, TILE, TILE), f32),
        in_specs=[any_space] * 6,
        out_specs=vmem,
        scratch_shapes=[
            wide, wide, wide, wide,
            pltpu.VMEM((2, 2, 5, 3 * TILE, HALF), f32),
            pltpu.VMEM((2, TILE, TILE), f32),
            pltpu.VMEM((2, TILE, TILE), f32),
            pltpu.VMEM(mats.shape, jnp.bfloat16),
            pltpu.VMEM(perms.shape, jnp.bfloat16),
            pltpu.VMEM((2, TILE, TILE), f32),
            field, field, field,
            pltpu.VMEM((2, 2, 4, HALF, HALF), f32),
            pltpu.VMEM((2, 2, 2, HALF, HALF), f32),
            pltpu.VMEM((2, 2, HALF, HALF), f32),
            pltpu.VMEM((2, 2, HALF, HALF), f32),
            pltpu.VMEM((2, 2, TILE, HALF), f32),
            pltpu.VMEM((2, 2, TILE, HALF), f32),
            pltpu.SMEM((1, 1, 2, 1, 2), jnp.int32),
            pltpu.SemaphoreType.DMA((9,)),
            pltpu.SemaphoreType.DMA((2, 12)),
            pltpu.SemaphoreType.DMA((2, 12)),
            pltpu.SemaphoreType.DMA((2, 8)),
            pltpu.SemaphoreType.DMA((2, 8)),
        ],
        compiler_params=pltpu.CompilerParams(
            collective_id=0, has_side_effects=True, vmem_limit_bytes=54 * 1024 * 1024
        ),
        cost_estimate=pl.CostEstimate(flops=3 * 10**9, bytes_accessed=8 * 10**6, transcendentals=131072),
    )(positions, obj, probe, amplitude.reshape(2, TILE, TILE), mats, perms)


def solution(mesh):
    mats, perms = constants()
    mats, perms = jnp.asarray(mats), jnp.asarray(perms)
    placed = (
        P(None, None, "row", "col"),
        P(),
        P("row", "col", None, None, None, None),
        P("row", "col", None, None, None),
    )
    return jax.shard_map(
        functools.partial(body, mesh.shape["row"], mesh.shape["col"], mats, perms),
        mesh=mesh, in_specs=placed, out_specs=P(None, None, "row", "col"), check_vma=False,
    )
```

```python
import functools
import math

import jax
import jax.numpy as jnp
import numpy as np
from jax import lax
from jax.experimental import pallas as pl
from jax.experimental.pallas import tpu as pltpu
from jax.sharding import PartitionSpec as P

TILE = 256
MARGIN = 128
HALF = 128
WIDE = 512
STEP = 0.5
MESH = pl.DeviceIdType.MESH

G_FX, G_FI, G_VX, G_VI, G_CROSS, G_CROSS2, G_DIRECT, G_FWD, G_IN, G_IN2, G_INF, G_INV = range(12)
S_CORNER, S_CROSS, S_DIRECT, S_IN, S_FX, S_FI, S_VX, S_VI = range(8)

T_A, T_F, T_FI, T_AC = range(4)


def real_form(m):
    return np.block([[m.real, m.imag], [-m.imag, m.real]])


def matrices():
    n = np.arange(TILE)
    f = np.where(n < TILE // 2, n, n - TILE)
    h = np.exp(-1j * math.pi * ((f * f) % (4 * TILE)) / (2 * TILE))
    dft = np.exp(-2j * math.pi * ((n[:, None] * n[None, :]) % TILE) / TILE) / math.sqrt(TILE)
    spread = np.conj(dft) @ (h[:, None] * dft)
    c0, c1 = spread[:HALF, :HALF], spread[:HALF, HALF:]
    a = [(c0 + c1) / 2, (c0 - c1) / 2]
    fwd = [dft[:HALF, 0::2], dft[:HALF, 1::2]]
    inv = [np.conj(m.T) for m in fwd]
    ac = [np.conj(m) for m in a]
    return np.stack([np.stack([real_form(m) for m in pair]) for pair in (a, fwd, inv, ac)])


def constants():
    right = matrices()
    both = np.stack([right, np.swapaxes(right, -1, -2)], 2)
    both = both.astype(np.float32)
    high = both.astype(jnp.bfloat16)
    low = (both - high.astype(np.float32)).astype(jnp.bfloat16)
    mats = np.stack([high, low], 3)
    order = np.concatenate([np.arange(0, TILE, 2), np.arange(1, TILE, 2)])
    perm = np.zeros((TILE, TILE), np.float32)
    perm[order, np.arange(TILE)] = 1.0
    perms = np.stack([perm, perm.T]).astype(jnp.bfloat16)
    return mats, perms


def split(x):
    high = x.astype(jnp.bfloat16)
    low = (x - high.astype(jnp.float32)).astype(jnp.bfloat16)
    return high, low


def dot(a, b):
    return jnp.dot(a, b, preferred_element_type=jnp.float32)


def mm_right(x, high, low):
    xh, xl = split(x)
    return dot(xh, high) + (dot(xl, high) + dot(xh, low))


def mm_left(high, low, x):
    xh, xl = split(x)
    return dot(high, xh) + (dot(high, xl) + dot(low, xh))


def transform(src, dst, mats, which, pre, post):
    sums, diffs = [], []
    for w in range(2):
        xr, xi = src[w, 0], src[w, 1]
        r0, r1, i0, i1 = xr[:, :HALF], xr[:, HALF:], xi[:, :HALF], xi[:, HALF:]
        if pre:
            r0, r1, i0, i1 = r0 + r1, r0 - r1, i0 + i1, i0 - i1
        sums.append(jnp.concatenate([r0, i0], 1))
        diffs.append(jnp.concatenate([r1, i1], 1))
    all_s = mm_right(jnp.concatenate(sums, 0), mats[which, 0, 0, 0], mats[which, 0, 0, 1])
    all_d = mm_right(jnp.concatenate(diffs, 0), mats[which, 1, 0, 0], mats[which, 1, 0, 1])
    for w in range(2):
        ys, yd = all_s[TILE * w : TILE * (w + 1)], all_d[TILE * w : TILE * (w + 1)]
        if post:
            ys, yd = ys + yd, ys - yd
        yr = jnp.concatenate([ys[:, :HALF], yd[:, :HALF]], 1)
        yi = jnp.concatenate([ys[:, HALF:], yd[:, HALF:]], 1)
        r0, r1, i0, i1 = yr[:HALF], yr[HALF:], yi[:HALF], yi[HALF:]
        if pre:
            r0, r1, i0, i1 = r0 + r1, r0 - r1, i0 + i1, i0 - i1
        zs = mm_left(mats[which, 0, 1, 0], mats[which, 0, 1, 1], jnp.concatenate([r0, i0], 0))
        zd = mm_left(mats[which, 1, 1, 0], mats[which, 1, 1, 1], jnp.concatenate([r1, i1], 0))
        if post:
            zs, zd = zs + zd, zs - zd
        dst[w, 0, :HALF, :] = zs[:HALF]
        dst[w, 0, HALF:, :] = zd[:HALF]
        dst[w, 1, :HALF, :] = zs[HALF:]
        dst[w, 1, HALF:, :] = zd[HALF:]


ROWS = 32


def rows_loop(count, fn):
    def step(k, carry):
        fn(pl.multiple_of(k * ROWS, ROWS))
        return carry

    lax.fori_loop(0, count // ROWS, step, 0, unroll=8 if count == TILE else 4)


def kernel(
    n_row, n_col,
    pos_any, obj_ref, probe_ref, amp_ref, mats_ref, perms_ref,
    out_ref,
    pad0, pad1, tot0, tot1, gbuf, probe, amp, mats, perms, amp_p, x_ref, b_ref, t_ref,
    r_in, r_x, r_c, r_d, r_f, r_v,
    pos_ref, local_sem, g_send, g_recv, s_send, s_recv,
):
    i, j = lax.axis_index("row"), lax.axis_index("col")
    core = lax.rem(i, 2)
    c = lax.rem(lax.div(i, 2), 2)
    i_in = i + 1 - 2 * core
    i_x = i - 1 + 2 * core
    j_v = j - 1 + 2 * c
    j_f = j + 1 - 2 * c
    has_x = jnp.logical_and(i_x >= 0, i_x < n_row)
    has_v = jnp.logical_and(j_v >= 0, j_v < n_col)
    has_f = jnp.logical_and(j_f >= 0, j_f < n_col)
    has_d = jnp.logical_and(has_x, has_v)
    ix = jnp.clip(i_x, 0, n_row - 1)
    jv = jnp.clip(j_v, 0, n_col - 1)
    jf = jnp.clip(j_f, 0, n_col - 1)
    always = None
    pads, tots = (pad0, pad1), (tot0, tot1)

    def at(start):
        return pl.ds(pl.multiple_of(start, HALF), HALF)

    x_rows, in_rows = at(HALF * core), at(HALF * (1 - core))
    x_rows_p, in_rows_p = at(MARGIN + HALF * core), at(MARGIN + HALF * (1 - core))

    barrier = pltpu.get_barrier_semaphore()

    def when(cond, fn):
        if cond is None:
            fn()
        else:
            pl.when(cond)(fn)

    partners = ((None, (i_in, j)), (has_x, (ix, j)), (has_d, (ix, jv)), (has_v, (i, jv)), (has_f, (i, jf)))
    for cond, dev in partners:
        when(cond, lambda dev=dev: pl.semaphore_signal(barrier, inc=1, device_id=dev, device_id_type=MESH))
    one = lambda cond: cond.astype(jnp.int32)
    pl.semaphore_wait(barrier, 1 + one(has_x) + one(has_d) + one(has_v) + one(has_f))

    def gather(s):
        pad = pads[s]
        dst_x, dst_in = at(3 * HALF * (1 - core)), at(3 * HALF * core)
        f_src, f_dst = at(HALF * (1 - c)), 3 * c
        v_src, v_dst = at(HALF * c), 3 * (1 - c)
        west, east = pl.ds(0, HALF), pl.ds(HALF, HALF)
        obj = obj_ref.at[s]
        table = {
            G_FX: (has_f, has_v, obj.at[:, x_rows, f_src], pad.at[:, f_dst, x_rows_p, :], (i, jf)),
            G_FI: (has_f, has_v, obj.at[:, in_rows, f_src], pad.at[:, f_dst, in_rows_p, :], (i, jf)),
            G_VX: (has_v, has_f, obj.at[:, x_rows, v_src], pad.at[:, v_dst, x_rows_p, :], (i, jv)),
            G_VI: (has_v, has_f, obj.at[:, in_rows, v_src], pad.at[:, v_dst, in_rows_p, :], (i, jv)),
            G_CROSS: (has_x, has_x, obj.at[:, x_rows, west], pad.at[:, 1, dst_x, :], (ix, j)),
            G_CROSS2: (has_x, has_x, obj.at[:, x_rows, east], pad.at[:, 2, dst_x, :], (ix, j)),
            G_DIRECT: (has_d, has_d, obj.at[:, x_rows, v_src], pad.at[:, v_dst, dst_x, :], (ix, jv)),
            G_FWD: (has_x, has_x, pad.at[:, f_dst, x_rows_p, :], pad.at[:, f_dst, dst_x, :], (ix, j)),
            G_IN: (always, always, obj.at[:, in_rows, west], pad.at[:, 1, dst_in, :], (i_in, j)),
            G_IN2: (always, always, obj.at[:, in_rows, east], pad.at[:, 2, dst_in, :], (i_in, j)),
            G_INF: (always, always, pad.at[:, f_dst, in_rows_p, :], pad.at[:, f_dst, dst_in, :], (i_in, j)),
            G_INV: (always, always, pad.at[:, v_dst, in_rows_p, :], pad.at[:, v_dst, dst_in, :], (i_in, j)),
        }
        return {
            k: (sent, comes, pltpu.make_async_remote_copy(
                src_ref=src, dst_ref=dst, send_sem=g_send.at[s, k], recv_sem=g_recv.at[s, k],
                device_id=dev, device_id_type=MESH))
            for k, (sent, comes, src, dst, dev) in table.items()
        }

    def start(copies, *keys):
        for k in keys:
            sent, _, copy = copies[k]
            when(sent, copy.start)

    def arrived(copies, *keys):
        for k in keys:
            _, comes, copy = copies[k]
            when(comes, copy.wait_recv)

    def left(copies, *keys):
        for k in keys:
            sent, _, copy = copies[k]
            when(sent, copy.wait_send)

    g0, g1 = gather(0), gather(1)
    inner_first = (G_FI, G_VI, G_IN, G_IN2)
    then = (G_CROSS, G_CROSS2, G_VX, G_DIRECT)
    start(g0, G_FX)
    start(g1, G_FX)
    start(g0, *inner_first, *then)

    inner = pl.ds(MARGIN, TILE)
    locals_ = [
        pltpu.make_async_copy(obj_ref.at[s, :, :, pl.ds(HALF * k, HALF)], pad.at[:, 1 + k, inner, :], local_sem.at[4 + 2 * s + k])
        for s, pad in enumerate(pads)
        for k in range(2)
    ] + [
        pltpu.make_async_copy(pos_any, pos_ref, local_sem.at[8]),
        pltpu.make_async_copy(probe_ref, probe, local_sem.at[0]),
        pltpu.make_async_copy(amp_ref, amp, local_sem.at[1]),
        pltpu.make_async_copy(mats_ref, mats, local_sem.at[2]),
        pltpu.make_async_copy(perms_ref, perms, local_sem.at[3]),
    ]
    for copy in locals_:
        copy.start()

    start(g1, *inner_first)

    def zero(cond, row0, count, blocks):
        def chunk(r):
            for pad in pads:
                for k in blocks:
                    pad[:, k, pl.ds(pl.multiple_of(row0 + r, ROWS), ROWS), :] = jnp.zeros((2, ROWS, HALF), jnp.float32)

        @pl.when(jnp.logical_not(cond))
        def _():
            rows_loop(count, chunk)

    zero(has_v, MARGIN, TILE, (3 * c,))
    zero(has_f, MARGIN, TILE, (3 * (1 - c),))
    zero(has_d, 3 * HALF * core, HALF, (3 * c,))
    zero(has_x, 3 * HALF * core, HALF, (1, 2, 3 * (1 - c)))

    def clear(r):
        for w in range(2):
            gbuf[w, :, :, pl.ds(r, ROWS), :] = jnp.zeros((2, 5, ROWS, HALF), jnp.float32)

    rows_loop(3 * TILE, clear)
    for copy in locals_[6:]:
        copy.wait()

    def order(w, carry):
        rest = amp[w]
        total = None
        for _ in range(3):
            piece = rest.astype(jnp.bfloat16)
            rest = rest - piece.astype(jnp.float32)
            part = dot(perms[1], dot(piece, perms[0]).astype(jnp.bfloat16))
            total = part if total is None else total + part
        amp_p[w] = total
        return carry

    for copies in (g0, g1):
        arrived(copies, G_FX)
        start(copies, G_FWD)
    lax.fori_loop(0, 2, order, 0)
    for copy in locals_[:6]:
        copy.wait()

    lane = lax.broadcasted_iota(jnp.int32, (ROWS, HALF), 1)

    def place(w):
        y, x = pos_ref[0, 0, w, 0, 0], pos_ref[0, 0, w, 0, 1]
        q = jnp.minimum(lax.div(x, HALF), 1)
        return y, q, x - q * HALF

    def window(pad, w, part, r):
        y, block, s = place(w)
        turn = lax.rem(HALF - s, HALF)
        v = [pltpu.roll(pad[part, block + k, pl.ds(y + r, ROWS), :], turn, 1) for k in range(3)]
        own = lane < HALF - s
        return jnp.concatenate([jnp.where(own, v[0], v[1]), jnp.where(own, v[1], v[2])], 1)

    def finish_gather(copies):
        arrived(copies, G_FI)
        start(copies, G_INF)
        arrived(copies, G_VI)
        start(copies, G_INV)
        arrived(copies, G_VX, G_CROSS, G_CROSS2, G_DIRECT, G_IN, G_IN2, G_FWD, G_INF, G_INV)

    finish_gather(g0)
    start(g1, *then)

    for w in range(2):
        def enter(r, w=w):
            rows = pl.ds(r, ROWS)
            tr, ti = 1.0 + window(pad0, w, 0, r), window(pad0, w, 1, r)
            pr, pi = probe[0, rows, :], probe[1, rows, :]
            x_ref[w, 0, rows, :] = pr * tr - pi * ti
            x_ref[w, 1, rows, :] = pr * ti + pi * tr

        rows_loop(TILE, enter)
    transform(x_ref, b_ref, mats, T_A, True, True)

    finish_gather(g1)

    for w in range(2):
        def leave(r, w=w):
            rows = pl.ds(r, ROWS)
            tr, ti = 1.0 + window(pad1, w, 0, r), window(pad1, w, 1, r)
            t_ref[w, 0, rows, :] = tr
            t_ref[w, 1, rows, :] = ti
            br, bi = b_ref[w, 0, rows, :], b_ref[w, 1, rows, :]
            x_ref[w, 0, rows, :] = br * tr - bi * ti
            x_ref[w, 1, rows, :] = br * ti + bi * tr

        rows_loop(TILE, leave)
    transform(x_ref, x_ref, mats, T_F, True, False)

    for w in range(2):
        def residual(r, w=w):
            rows = pl.ds(r, ROWS)
            fr, fi = x_ref[w, 0, rows, :], x_ref[w, 1, rows, :]
            keep = 1.0 - amp_p[w, rows, :] * lax.rsqrt(fr * fr + fi * fi + 1.0)
            x_ref[w, 0, rows, :] = fr * keep
            x_ref[w, 1, rows, :] = fi * keep

        rows_loop(TILE, residual)
    transform(x_ref, x_ref, mats, T_FI, False, True)

    def turned(w, part, r, v):
        _, _, s = place(w)
        turn = lax.rem(s, HALF)
        a, b = (pltpu.roll(v[:, HALF * k : HALF * (k + 1)], turn, 1) for k in range(2))
        own = lane >= s
        rows = pl.ds(TILE + r, ROWS)
        gbuf[w, part, 1, rows, :] = jnp.where(own, a, 0.0)
        gbuf[w, part, 2, rows, :] = jnp.where(own, b, a)
        gbuf[w, part, 3, rows, :] = jnp.where(own, 0.0, b)

    def add_up(tot, row0, count, blocks):
        def chunk(r):
            r = pl.multiple_of(row0 + r, ROWS)
            for part in range(2):
                for k in blocks:
                    total = None
                    for w in range(2):
                        y, block, _ = place(w)
                        v = gbuf[w, part, 1 - block + k, pl.ds(TILE - y + r, ROWS), :]
                        total = v if total is None else total + v
                    tot[part, k, pl.ds(r, ROWS), :] = total

        rows_loop(count, chunk)

    def scatter(s):
        tot = tots[s]
        cross_rows, inner_rows = at(3 * HALF * core), at(3 * HALF * (1 - core))
        f_blk, v_blk = 3 * (1 - c), 3 * c
        table = {
            S_CORNER: (has_x, has_x, tot.at[:, f_blk, cross_rows, :], r_c.at[s], (ix, j)),
            S_CROSS: (has_x, has_x, tot.at[:, pl.ds(1, 2), cross_rows, :], r_x.at[s], (ix, j)),
            S_DIRECT: (has_d, has_d, tot.at[:, v_blk, cross_rows, :], r_d.at[s], (ix, jv)),
            S_IN: (always, always, tot.at[:, :, inner_rows, :], r_in.at[s], (i_in, j)),
            S_FX: (has_f, has_v, tot.at[:, f_blk, x_rows_p, :], r_f.at[s, :, x_rows, :], (i, jf)),
            S_FI: (has_f, has_v, tot.at[:, f_blk, in_rows_p, :], r_f.at[s, :, in_rows, :], (i, jf)),
            S_VX: (has_v, has_f, tot.at[:, v_blk, x_rows_p, :], r_v.at[s, :, x_rows, :], (i, jv)),
            S_VI: (has_v, has_f, tot.at[:, v_blk, in_rows_p, :], r_v.at[s, :, in_rows, :], (i, jv)),
        }
        return {
            k: (sent, comes, pltpu.make_async_remote_copy(
                src_ref=src, dst_ref=dst, send_sem=s_send.at[s, k], recv_sem=s_recv.at[s, k],
                device_id=dev, device_id_type=MESH))
            for k, (sent, comes, src, dst, dev) in table.items()
        }

    def add_in(s):
        tot = tots[s]

        def chunk(r):
            rows = pl.ds(pl.multiple_of(MARGIN + HALF * (1 - core) + r, ROWS), ROWS)
            tot[:, :, rows, :] = tot[:, :, rows, :] + r_in[s, :, :, pl.ds(r, ROWS), :]

        rows_loop(HALF, chunk)

    def add_corner(s):
        tot = tots[s]

        def chunk(r):
            rows = pl.ds(pl.multiple_of(MARGIN + HALF * core + r, ROWS), ROWS)
            tot[:, 3 * c, rows, :] = tot[:, 3 * c, rows, :] + r_c[s, :, pl.ds(r, ROWS), :]

        @pl.when(has_x)
        def _():
            rows_loop(HALF, chunk)

    def send_early(s, copies):
        everywhere = range(4)
        add_up(tots[s], 3 * HALF * core, HALF, everywhere)
        start(copies, S_CORNER, S_DIRECT)
        if s == 1:
            start(copies, S_CROSS)
        add_up(tots[s], MARGIN, TILE, (0, 3))
        start(copies, S_FX)
        add_up(tots[s], 3 * HALF * (1 - core), HALF, everywhere)
        start(copies, S_IN)
        add_up(tots[s], MARGIN, TILE, (1, 2))

    def send_inner(s, copies):
        arrived(copies, S_IN)
        add_in(s)
        start(copies, S_FI, S_VI)

    def send_late(s, copies):
        arrived(copies, S_CORNER)
        add_corner(s)
        start(copies, S_VX)

    def own_part(s):
        def chunk(r):
            rows, rows_p = pl.ds(r, ROWS), pl.ds(MARGIN + r, ROWS)
            for k in range(2):
                cols = slice(HALF * k, HALF * (k + 1))
                out_ref[s, :, rows, cols] = pads[s][:, 1 + k, rows_p, :] - STEP * tots[s][:, 1 + k, rows_p, :]

        rows_loop(TILE, chunk)

    def take(s, copies, key, cond, rows0, cols, part):
        if key is not None:
            arrived(copies, key)

        def chunk(r):
            rows = pl.ds(pl.multiple_of(rows0 + r, ROWS), ROWS)
            out_ref[s, :, rows, cols] = out_ref[s, :, rows, cols] - STEP * part(r)

        @pl.when(cond)
        def _():
            rows_loop(HALF, chunk)

    def finish(s, copies):
        x0, in0 = HALF * core, HALF * (1 - core)
        f_cols, v_cols = at(HALF * c), at(HALF * (1 - c))
        west, east = slice(0, HALF), slice(HALF, TILE)
        take(s, copies, S_DIRECT, has_d, x0, f_cols, lambda r: r_d[s, :, pl.ds(r, ROWS), :])
        take(s, copies, S_CROSS, has_x, x0, west, lambda r: r_x[s, :, 0, pl.ds(r, ROWS), :])
        take(s, copies, None, has_x, x0, east, lambda r: r_x[s, :, 1, pl.ds(r, ROWS), :])
        take(s, copies, S_FX, has_v, x0, f_cols, lambda r: r_f[s, :, pl.ds(pl.multiple_of(x0 + r, ROWS), ROWS), :])
        take(s, copies, S_FI, has_v, in0, f_cols, lambda r: r_f[s, :, pl.ds(pl.multiple_of(in0 + r, ROWS), ROWS), :])
        take(s, copies, S_VI, has_f, in0, v_cols, lambda r: r_v[s, :, pl.ds(pl.multiple_of(in0 + r, ROWS), ROWS), :])
        take(s, copies, S_VX, has_f, x0, v_cols, lambda r: r_v[s, :, pl.ds(pl.multiple_of(x0 + r, ROWS), ROWS), :])

    for w in range(2):
        def second(r, w=w):
            rows = pl.ds(r, ROWS)
            br, bi = b_ref[w, 0, rows, :], b_ref[w, 1, rows, :]
            cr, ci = x_ref[w, 0, rows, :], x_ref[w, 1, rows, :]
            turned(w, 0, r, br * cr + bi * ci)
            turned(w, 1, r, br * ci - bi * cr)

        rows_loop(TILE, second)
    s1 = scatter(1)
    send_early(1, s1)

    for w in range(2):
        def back(r, w=w):
            rows = pl.ds(r, ROWS)
            tr, ti = t_ref[w, 0, rows, :], t_ref[w, 1, rows, :]
            cr, ci = x_ref[w, 0, rows, :], x_ref[w, 1, rows, :]
            x_ref[w, 0, rows, :] = tr * cr + ti * ci
            x_ref[w, 1, rows, :] = tr * ci - ti * cr

        rows_loop(TILE, back)
    send_inner(1, s1)
    send_late(1, s1)
    transform(x_ref, x_ref, mats, T_AC, True, True)
    for w in range(2):
        def first_slice(r, w=w):
            rows = pl.ds(r, ROWS)
            pr, pi = probe[0, rows, :], probe[1, rows, :]
            cr, ci = x_ref[w, 0, rows, :], x_ref[w, 1, rows, :]
            turned(w, 0, r, pr * cr + pi * ci)
            turned(w, 1, r, pr * ci - pi * cr)

        rows_loop(TILE, first_slice)
    s0 = scatter(0)
    send_early(0, s0)
    send_inner(0, s0)
    left(s1, S_CROSS)
    start(s0, S_CROSS)
    send_late(0, s0)
    own_part(1)
    own_part(0)
    finish(1, s1)
    finish(0, s0)
    for copies in (g0, g1, s0):
        left(copies, *copies)
    left(s1, *(k for k in s1 if k not in (S_CROSS,)))


def body(n_row, n_col, mats, perms, obj, probe, amplitude, positions):
    any_space = pl.BlockSpec(memory_space=pltpu.HBM)
    vmem = pl.BlockSpec(memory_space=pltpu.VMEM)
    f32 = jnp.float32
    wide = pltpu.VMEM((2, 4, WIDE, HALF), f32)
    field = pltpu.VMEM((2, 2, TILE, TILE), f32)
    return pl.pallas_call(
        functools.partial(kernel, n_row, n_col),
        out_shape=pltpu.VMEM((2, 2, TILE, TILE), f32),
        in_specs=[any_space] * 6,
        out_specs=vmem,
        scratch_shapes=[
            wide, wide, wide, wide,
            pltpu.VMEM((2, 2, 5, 3 * TILE, HALF), f32),
            pltpu.VMEM((2, TILE, TILE), f32),
            pltpu.VMEM((2, TILE, TILE), f32),
            pltpu.VMEM(mats.shape, jnp.bfloat16),
            pltpu.VMEM(perms.shape, jnp.bfloat16),
            pltpu.VMEM((2, TILE, TILE), f32),
            field, field, field,
            pltpu.VMEM((2, 2, 4, HALF, HALF), f32),
            pltpu.VMEM((2, 2, 2, HALF, HALF), f32),
            pltpu.VMEM((2, 2, HALF, HALF), f32),
            pltpu.VMEM((2, 2, HALF, HALF), f32),
            pltpu.VMEM((2, 2, TILE, HALF), f32),
            pltpu.VMEM((2, 2, TILE, HALF), f32),
            pltpu.SMEM((1, 1, 2, 1, 2), jnp.int32),
            pltpu.SemaphoreType.DMA((9,)),
            pltpu.SemaphoreType.DMA((2, 12)),
            pltpu.SemaphoreType.DMA((2, 12)),
            pltpu.SemaphoreType.DMA((2, 8)),
            pltpu.SemaphoreType.DMA((2, 8)),
        ],
        compiler_params=pltpu.CompilerParams(
            collective_id=0, has_side_effects=True, vmem_limit_bytes=54 * 1024 * 1024
        ),
        cost_estimate=pl.CostEstimate(flops=3 * 10**9, bytes_accessed=8 * 10**6, transcendentals=131072),
    )(positions, obj, probe, amplitude.reshape(2, TILE, TILE), mats, perms)


def solution(mesh):
    mats, perms = constants()
    mats, perms = jnp.asarray(mats), jnp.asarray(perms)
    placed = (
        P(None, None, "row", "col"),
        P(),
        P("row", "col", None, None, None, None),
        P("row", "col", None, None, None),
    )
    return jax.shard_map(
        functools.partial(body, mesh.shape["row"], mesh.shape["col"], mats, perms),
        mesh=mesh, in_specs=placed, out_specs=P(None, None, "row", "col"), check_vma=False,
    )
```
